256 devices in a mesh: seq: 64 (over y, z, core), head: 4 (over x).
Axes of the slice: x: 4, y: 4, z: 8, core: 2. Of those that a mesh axis runs over, the one named last changes fastest.
Arguments:
- queries: bfloat16 [131072, 512], P('seq', 'head'), may hold values from -6 to 6
- keys: bfloat16 [131072, 512], P('seq', 'head'), may hold values from -6 to 6
- values: bfloat16 [131072, 512], P('seq', 'head'), may hold values from -6 to 6
- delta: float32 [8, 131072], P('head', 'seq'), may hold values from -36 to 36
- dout: bfloat16 [131072, 512], P('seq', 'head'), may hold values from -48 to 48
- partner: int32 [512], P('seq'), may hold values from 0 to 511, as said below
- sort_weight: float32 [8, 64, 64], P('head'), may hold values from -0.75 to 0.75
Outputs:
- d_queries: bfloat16 [131072, 512], P('seq', 'head')
- d_keys: bfloat16 [131072, 512], P('seq', 'head')
- d_values: bfloat16 [131072, 512], P('seq', 'head')
- d_sort: float32 [8, 64, 64], P('head')
The draws below stay inside these ranges and needn't reach their ends.
Inputs may be any that keep to these rules, and one draw needn't show every extreme that they name: partner is a permutation of the 512 blocks; the blocks of one index of seq are 8 consecutive ones, and no block's partner lies on the same index; of the blocks of one index at most 1 have partners on one other index, and every index reaches 8 others.
All inputs are finite; a program needn't handle non-finite values.
Results may differ from the reference program's by a relative error of at most 0.0095.
Values may be sent and summed in bfloat16 or wider, within the bound.
No kernel may reach another device: no remote copies, remote signals or barrier semaphores. Data moves between devices by JAX's collectives and lax.ppermute only.
A program may use at most 128 MiB of HBM per device.

```python
import math
import jax
import jax.numpy as jnp
from jax import lax

HEADS = 8
HD = 64
BLOCK_LEN = 256
BLK_DEV = 8
BLOCKS = 512
TOKENS = 131072
FEATS = 512


def draw_queries(key, part):
    key = jax.random.fold_in(key, 1)
    value = jnp.clip(jax.random.normal(key, (TOKENS, FEATS), jnp.float32), -6.0, 6.0)
    return value.astype(jnp.bfloat16)


def draw_keys(key, part):
    key = jax.random.fold_in(key, 2)
    value = jnp.clip(jax.random.normal(key, (TOKENS, FEATS), jnp.float32), -6.0, 6.0)
    return value.astype(jnp.bfloat16)


def draw_partner(key, part):
    key = jax.random.fold_in(key, 3)
    seq_count = BLOCKS // BLK_DEV
    group_size = (BLK_DEV + seq_count - 2) // (seq_count - 1)
    offsets = jax.random.permutation(jax.random.fold_in(key, 1), seq_count - 1).astype(jnp.int32) + 1
    grouping = jax.random.permutation(jax.random.fold_in(key, 2), BLK_DEV).astype(jnp.int32)
    landing = jax.random.permutation(jax.random.fold_in(key, 3), BLK_DEV).astype(jnp.int32)
    relabel = jax.random.permutation(jax.random.fold_in(key, 4), seq_count).astype(jnp.int32)
    inverse = jnp.zeros((seq_count,), jnp.int32).at[relabel].set(jnp.arange(seq_count, dtype=jnp.int32))
    slot_offset = offsets[grouping // group_size]
    moved = (inverse[:, None] + slot_offset[None, :]) % seq_count
    owner = relabel[moved]
    table = owner * BLK_DEV + landing[None, :]
    return table.reshape(BLOCKS).astype(jnp.int32)


def levels(key, dims, split, smallest, largest):
    def one(dim, shards_of):
        draws = jax.random.uniform(jax.random.fold_in(jax.random.fold_in(key, 6), dim), (shards_of,), jnp.float32, smallest / len(split), largest / len(split))
        return jnp.repeat(jnp.exp(draws), dims[dim] // shards_of).reshape((-1,) + (1,) * (len(dims) - dim - 1))

    gain = one(*split[0])
    for cut in split[1:]:
        gain = gain * one(*cut)
    return gain


def noise(stream_key, dims, width, limit, cuts=(), held_as=jnp.bfloat16):
    drawn = width * jax.random.normal(stream_key, dims, jnp.float32)
    if cuts:
        drawn = drawn * levels(stream_key, dims, cuts, -0.22, 0.18)
    return jnp.clip(drawn, -limit, limit).astype(held_as)


def setup_inputs(seed: int = 0) -> dict:
    arg_keys = jax.random.split(jax.random.key(seed), 8)
    return {
        "queries": draw_queries(jax.random.fold_in(arg_keys[7], 71), 0),
        "keys": draw_keys(jax.random.fold_in(arg_keys[7], 71), 0),
        "values": noise(arg_keys[2], (TOKENS, FEATS), 1.0, 6.0, ((0, 64), (1, 4))),
        "delta": noise(arg_keys[3], (HEADS, TOKENS), 6.0, 36.0, ((0, 4), (1, 64)), jnp.float32),
        "dout": noise(arg_keys[4], (TOKENS, FEATS), 8.0, 48.0, ((0, 64), (1, 4))),
        "partner": draw_partner(jax.random.fold_in(arg_keys[7], 71), 0),
        "sort_weight": noise(arg_keys[6], (HEADS, HD, HD), HD ** -0.5, 0.75, ((0, 4),), jnp.float32),
    }


def block_terms(items):
    q_blk, k_blk, v_blk, delta, g_blk, k_far, v_far, summ_far, sortq_own = items
    score_scale = 1.0 / math.sqrt(HD)
    q32 = q_blk.astype(jnp.float32)
    k32 = k_blk.astype(jnp.float32)
    v32 = v_blk.astype(jnp.float32)
    g32 = g_blk.astype(jnp.float32)
    kf32 = k_far.astype(jnp.float32)
    vf32 = v_far.astype(jnp.float32)
    s_self = jnp.einsum('bqhd,bkhd->bhqk', q32, k32) * score_scale
    s_far = jnp.einsum('bqhd,bkhd->bhqk', q32, kf32) * score_scale
    joint_max = jnp.maximum(lax.optimization_barrier(jnp.max(s_self, axis=3)), lax.optimization_barrier(jnp.max(s_far, axis=3)))
    joint_total = lax.optimization_barrier(jnp.sum(jnp.exp(s_self - joint_max[..., None]), axis=3)) + lax.optimization_barrier(jnp.sum(jnp.exp(s_far - joint_max[..., None]), axis=3))
    log_total = joint_max + jnp.log(joint_total)
    p_self = jnp.exp(s_self - log_total[..., None])
    p_far = jnp.exp(s_far - log_total[..., None])
    low_self = p_self.astype(jnp.bfloat16).astype(jnp.float32)
    low_far = p_far.astype(jnp.bfloat16).astype(jnp.float32)
    gates = jax.nn.sigmoid(score_scale * lax.optimization_barrier(jnp.sum(sortq_own * summ_far, axis=2)))
    grad_self = jnp.einsum('bqhd,bkhd->bhqk', g32, v32)
    grad_far = jnp.einsum('bqhd,bkhd->bhqk', g32, vf32)
    gate_grad = lax.optimization_barrier(jnp.sum(low_far * grad_far, axis=(2, 3)))
    ds_self = (p_self * (grad_self - delta[..., None])).astype(jnp.bfloat16).astype(jnp.float32)
    ds_far = (p_far * (gates[:, :, None, None] * grad_far - delta[..., None])).astype(jnp.bfloat16).astype(jnp.float32)
    dq_far = (score_scale * jnp.einsum('bhqk,bkhd->bqhd', ds_far, kf32)).astype(jnp.bfloat16)
    d_queries = (score_scale * jnp.einsum('bhqk,bkhd->bqhd', ds_self, k32) + dq_far.astype(jnp.float32)).astype(jnp.bfloat16)
    dk_self = score_scale * jnp.einsum('bhqk,bqhd->bkhd', ds_self, q32)
    dk_far = (score_scale * jnp.einsum('bhqk,bqhd->bkhd', ds_far, q32)).astype(jnp.bfloat16)
    dv_self = jnp.einsum('bhqk,bqhd->bkhd', low_self, g32)
    dv_far = (gates[:, None, :, None] * jnp.einsum('bhqk,bqhd->bkhd', low_far, g32)).astype(jnp.bfloat16)
    logit_grad = gate_grad * gates * (1.0 - gates)
    sortq_grad = score_scale * logit_grad[..., None] * summ_far
    column_grad = score_scale * logit_grad[..., None] * sortq_own
    return (d_queries, dk_self, dv_self, dk_far, dv_far, sortq_grad, column_grad)

def reference(queries, keys, values, delta, dout, partner, sort_weight):
    block_shape = (BLOCKS, BLOCK_LEN, HEADS, HD)
    pool_scale = 1.0 / math.sqrt(BLOCK_LEN)
    q_blocks = queries.reshape(block_shape)
    k_blocks = keys.reshape(block_shape)
    v_blocks = values.reshape(block_shape)
    g_blocks = dout.reshape(block_shape)
    delta_blocks = jnp.transpose(delta.reshape(HEADS, BLOCKS, BLOCK_LEN), (1, 0, 2))
    summary = lax.optimization_barrier(jnp.sum(k_blocks.astype(jnp.float32), axis=1)) * pool_scale
    sortq = jnp.einsum('bhd,hde->bhe', summary, sort_weight, precision=lax.Precision.HIGHEST)
    members = (q_blocks, k_blocks, v_blocks, delta_blocks, g_blocks, k_blocks[partner], v_blocks[partner], summary[partner], sortq)
    grouped = tuple((member.reshape((BLOCKS // BLK_DEV, BLK_DEV) + member.shape[1:]) for member in members))
    results = lax.map(block_terms, grouped)
    flat = tuple((result.reshape((BLOCKS,) + result.shape[2:]) for result in results))
    d_queries, dk_self, dv_self, dk_far, dv_far, sortq_grad, column_grad = flat
    dk_owned = jnp.zeros_like(dk_far).at[partner].set(dk_far)
    dv_owned = jnp.zeros_like(dv_far).at[partner].set(dv_far)
    column_owned = jnp.zeros_like(column_grad).at[partner].set(column_grad)
    row_grad = jnp.einsum('bhe,hde->bhd', sortq_grad, sort_weight, precision=lax.Precision.HIGHEST)
    d_keys = (dk_self + dk_owned.astype(jnp.float32) + pool_scale * (row_grad + column_owned)[:, None]).astype(jnp.bfloat16)
    d_values = (dv_self + dv_owned.astype(jnp.float32)).astype(jnp.bfloat16)
    d_sort = jnp.einsum('bhd,bhe->hde', summary, sortq_grad, precision=lax.Precision.HIGHEST)
    return (d_queries.reshape(TOKENS, FEATS), d_keys.reshape(TOKENS, FEATS), d_values.reshape(TOKENS, FEATS), d_sort)
```

```python
import functools
import math

import jax
import jax.numpy as jnp
from jax import lax
from jax.experimental import pallas as pl
from jax.experimental.pallas import tpu as pltpu
from jax.sharding import PartitionSpec as P

F32 = jnp.float32
BF16 = jnp.bfloat16
LANES = 128
HALF = 64
SHARE_AT = 64
VMEM_LIMIT = 48 * 1024 * 1024


def dot(a, b, dims, **kw):
    return lax.dot_general(a, b, (dims, ((), ())), preferred_element_type=F32, **kw)


def head_stack(x, scale):
    lane = lax.broadcasted_iota(jnp.int32, x.shape, 1)
    x32 = x.astype(F32) * scale
    first = jnp.where(lane < HALF, x32, 0.0)
    second = jnp.where(lane < HALF, 0.0, x32)
    return jnp.concatenate([first, second], axis=0).astype(BF16)


def split3(x):
    high = x.astype(BF16).astype(F32)
    rest = x - high
    mid = rest.astype(BF16).astype(F32)
    return high, mid, (rest - mid).astype(BF16).astype(F32)


def to_rows(v):
    return jnp.concatenate([v[:, i * HALF : (i + 1) * HALF] for i in range(8)], axis=0)


def from_rows(x):
    return jnp.concatenate([x[i : i + 1, :] for i in range(8)], axis=1)


def head_rows(v):
    return jnp.concatenate([v[:, :HALF], v[:, HALF:]], axis=0)


def from_head_rows(x):
    return jnp.concatenate([x[0:1, :], x[1:2, :]], axis=1)


def block_diagonal(w_ref):
    zero = jnp.zeros((HALF, HALF), F32)
    top = jnp.concatenate([w_ref[0], zero], axis=1)
    bottom = jnp.concatenate([zero, w_ref[1]], axis=1)
    return jnp.concatenate([top, bottom], axis=0)


def head_sums(x):
    lane = lax.broadcasted_iota(jnp.int32, x.shape, 1)
    first = jnp.sum(jnp.where(lane < HALF, x, 0.0), axis=1, keepdims=True)
    second = jnp.sum(jnp.where(lane < HALF, 0.0, x), axis=1, keepdims=True)
    return jnp.where(lane < HALF, first, second)


def reorder(rows_ref, source_ref, pieces, blocks, to_blocks):
    total = pieces * blocks
    out_row = lax.broadcasted_iota(jnp.int32, (total, total), 0)
    in_row = lax.broadcasted_iota(jnp.int32, (total, total), 1)
    if to_blocks:
        wanted = (out_row & (pieces - 1)) * blocks + (out_row >> 6)
    else:
        wanted = (out_row & (blocks - 1)) * pieces + (out_row >> 3)
    pick = jnp.where(wanted == in_row, 1.0, 0.0).astype(BF16)
    width = source_ref.shape[1]
    for start in range(0, width, 256):
        stop = min(width, start + 256)
        rows_ref[:, start:stop] = dot(pick, source_ref[:, start:stop], ((1,), (0,))).astype(BF16)


def fold(block, pieces):
    return jnp.concatenate(
        [block[c * pieces : (c + 1) * pieces, :] for c in range(block.shape[0] // pieces)], axis=1
    )


def unfold(rows):
    return jnp.concatenate(
        [rows[:, c * LANES : (c + 1) * LANES] for c in range(rows.shape[1] // LANES)], axis=0
    )


def pack_kernel(partner_ref, q_ref, k_ref, g_ref, delta_ref, out_ref, summary_ref, rows_ref):
    blocks, pieces, block_len = 8, 64, 256
    score_scale = 1.0 / math.sqrt(HALF)
    pool_scale = 1.0 / math.sqrt(block_len)

    def step(j, carry):
        at = pl.ds(pl.multiple_of(j * block_len, block_len), block_len)
        qb, kb, gb = q_ref[at, :], k_ref[at, :], g_ref[at, :]
        scores = dot(kb, head_stack(qb, score_scale), ((1,), (1,)))
        top = jnp.max(scores, axis=0, keepdims=True)
        lse = top + jnp.log(jnp.sum(jnp.exp(scores - top), axis=0, keepdims=True))
        summary = jnp.sum(kb.astype(F32), axis=0, keepdims=True) * pool_scale
        summary_ref[pl.ds(j, 1), :] = summary
        delta = jnp.concatenate([delta_ref[0:1, at], delta_ref[1:2, at]], axis=1)
        stats = jnp.concatenate([to_rows(lse), to_rows(delta)], axis=0)
        parts = jnp.concatenate(split3(stats), axis=0)
        summary_parts = jnp.concatenate(
            list(split3(head_rows(summary))) + [jnp.zeros((10, HALF), F32)], axis=0
        )
        left = jnp.concatenate([parts, summary_parts], axis=0)
        lane = lax.broadcasted_iota(jnp.int32, (pieces, HALF), 1)
        place = partner_ref[j]
        right = jnp.where(
            lane == 0,
            (place // 8).astype(F32),
            jnp.where(lane == 1, (place % 8).astype(F32), 0.0),
        )
        to = pl.ds(pl.multiple_of(j * pieces, pieces), pieces)
        rows_ref[to, 0:512] = fold(qb, pieces)
        rows_ref[to, 512:1024] = fold(gb, pieces)
        rows_ref[to, 1024:1152] = jnp.concatenate([left, right], axis=1).astype(BF16)
        return carry

    lax.fori_loop(0, blocks, step, 0)
    reorder(out_ref, rows_ref, pieces, blocks, False)


def partner_pick(tags):
    rows = tags.shape[0]
    place = tags[:, HALF : HALF + 1].astype(F32) * 8.0 + tags[:, HALF + 1 : HALF + 2].astype(F32)
    lane = lax.broadcasted_iota(jnp.int32, (rows, rows), 1).astype(F32)
    return jnp.where(lane == place, 1.0, 0.0).astype(BF16)


def forward_kernel(in_ref, out_ref):
    pick = partner_pick(in_ref[:, 1024:1152])
    for start in range(0, 1152, 256):
        stop = min(1152, start + 256)
        out_ref[:, start:stop] = dot(pick, in_ref[:, start:stop], ((0,), (0,))).astype(BF16)


def backward_kernel(tags_ref, in_ref, out_ref):
    pick = partner_pick(tags_ref[...])
    for start in (0, 256):
        out_ref[:, start : start + 256] = dot(
            pick, in_ref[:, start : start + 256], ((1,), (0,))
        ).astype(BF16)
    tail = in_ref[:, 512:640]
    moved = dot(pick, tail, ((1,), (0,)))
    rows = tail.shape[0]
    total = jnp.sum(tail.astype(F32).reshape(rows // 8, 8, LANES), axis=0)
    lane8 = lax.broadcasted_iota(jnp.int32, (8, LANES), 1)
    total = total + pltpu.roll(total, LANES - 16, 1) + pltpu.roll(total, LANES - 32, 1)
    total = jnp.where((lane8 >= SHARE_AT) & (lane8 < SHARE_AT + 16), total, 0.0)
    high, mid, low = split3(total)
    share = high + pltpu.roll(mid, 16, 1) + pltpu.roll(low, 32, 1)
    share = jnp.broadcast_to(share[None], (rows // 8, 8, LANES)).reshape(rows, LANES)
    lane = lax.broadcasted_iota(jnp.int32, (rows, LANES), 1)
    out_ref[:, 512:640] = jnp.where(lane < SHARE_AT, moved, share).astype(BF16)


def far_kernel(
    in_ref,
    k_ref,
    v_ref,
    summary_ref,
    w_ref,
    out_ref,
    dk_ref,
    dv_ref,
    column_ref,
    rows_ref,
    back_ref,
    gate_ref,
    grad_ref,
):
    blocks, pieces, block_len = 8, 64, 256
    score_scale = 1.0 / math.sqrt(HALF)
    reorder(rows_ref, in_ref, pieces, blocks, True)
    arrived = []
    for j in range(blocks):
        s = rows_ref[j * pieces + 48 : j * pieces + 64, 1024:1152].astype(F32)[:, :HALF]
        arrived.append(from_head_rows(s[0:2] + s[2:4] + s[4:6]))
    summary_in = jnp.concatenate(arrived, axis=0)
    summary = summary_ref[...]
    sortq = dot(summary_in, block_diagonal(w_ref), ((1,), (0,)), precision=lax.Precision.HIGHEST)
    gates = jax.nn.sigmoid(score_scale * head_sums(sortq * summary))
    gate_ref[...] = gates

    def step(j, carry):
        at = pl.ds(pl.multiple_of(j * block_len, block_len), block_len)
        here = pl.ds(pl.multiple_of(j * pieces, pieces), pieces)
        kb, vb = k_ref[at, :], v_ref[at, :]
        qs = head_stack(unfold(rows_ref[here, 0:512]), score_scale)
        gs = head_stack(unfold(rows_ref[here, 512:1024]), 1.0)
        stats = rows_ref[here, 1024:1152].astype(F32)
        joined = stats[0:16, :HALF] + stats[16:32, :HALF] + stats[32:48, :HALF]
        own_lse = from_rows(joined[0:8])
        delta = from_rows(joined[8:16])
        gate = gate_ref[pl.ds(j, 1), :]
        gate_row = jnp.concatenate(
            [
                jnp.broadcast_to(gate[:, 0:1], (1, block_len)),
                jnp.broadcast_to(gate[:, HALF : HALF + 1], (1, block_len)),
            ],
            axis=1,
        )
        scores = dot(kb, qs, ((1,), (1,)))
        top = jnp.maximum(own_lse, jnp.max(scores, axis=0, keepdims=True))
        weights = jnp.exp(scores - top)
        total = jnp.exp(own_lse - top) + jnp.sum(weights, axis=0, keepdims=True)
        probs = weights * (1.0 / total)
        lse = top + jnp.log(total)
        low = probs.astype(BF16)
        dprobs = dot(vb, gs, ((1,), (1,)))
        gate_terms = jnp.sum(low.astype(F32) * dprobs, axis=0, keepdims=True)
        first = jnp.sum(gate_terms[:, :block_len], axis=1, keepdims=True)
        second = jnp.sum(gate_terms[:, block_len:], axis=1, keepdims=True)
        lane = lax.broadcasted_iota(jnp.int32, (1, LANES), 1)
        grad_ref[pl.ds(j, 1), :] = jnp.where(lane < HALF, first, second)
        dscores = (probs * (gate_row * dprobs - delta)).astype(BF16)
        dk_ref[at, :] = dot(dscores, qs, ((1,), (0,))).astype(BF16)
        dv_ref[at, :] = (dot(low, gs, ((1,), (0,))) * gate).astype(BF16)
        dq = dot(kb, dscores, ((0,), (0,))) * score_scale
        dq = jnp.concatenate([dq[:HALF, :block_len], dq[HALF:, block_len:]], axis=1)
        back_ref[here, 0:512] = dq.astype(BF16)
        parts = jnp.concatenate(
            list(split3(to_rows(lse))) + [jnp.zeros((pieces - 24, HALF), F32)], axis=0
        )
        back_ref[here, 512:640] = jnp.concatenate(
            [parts, jnp.zeros((pieces, HALF), F32)], axis=1
        ).astype(BF16)
        return carry

    lax.fori_loop(0, blocks, step, 0)
    logit_grad = grad_ref[...] * gates * (1.0 - gates)
    sortq_grad = score_scale * logit_grad * summary
    column_ref[...] = score_scale * logit_grad * sortq
    for j in range(blocks):
        parts = jnp.concatenate(
            list(split3(head_rows(sortq_grad[j : j + 1, :]))) + [jnp.zeros((10, HALF), F32)],
            axis=0,
        )
        back_ref[j * pieces + 32 : j * pieces + 48, 512:640] = jnp.concatenate(
            [parts, jnp.zeros((16, HALF), F32)], axis=1
        ).astype(BF16)
    reorder(out_ref, back_ref, pieces, blocks, False)
    outer = dot(summary_in, sortq_grad, ((0,), (0,)), precision=lax.Precision.HIGHEST)
    lane = lax.broadcasted_iota(jnp.int32, (LANES, LANES), 1)
    row = lax.broadcasted_iota(jnp.int32, (LANES, LANES), 0)
    outer = jnp.where(row < HALF, outer, pltpu.roll(outer, HALF, 1))
    inside = (lane >= SHARE_AT) & (lane < SHARE_AT + 16)
    for a in range(4):
        part = jnp.where(inside, pltpu.roll(outer, (SHARE_AT - 16 * a) % LANES, 1), 0.0)
        high, mid, low = split3(part)
        share = high + pltpu.roll(mid, 16, 1) + pltpu.roll(low, 32, 1)
        rows = slice(a * LANES, (a + 1) * LANES)
        out_ref[rows, 512:640] = (out_ref[rows, 512:640].astype(F32) + share).astype(BF16)


def self_kernel(
    in_ref,
    q_ref,
    k_ref,
    v_ref,
    g_ref,
    delta_ref,
    w_ref,
    dk_far_ref,
    dv_far_ref,
    column_ref,
    dq_out,
    dk_out,
    dv_out,
    sort_out,
    rows_ref,
    extra_ref,
):
    blocks, pieces, block_len = 8, 64, 256
    score_scale = 1.0 / math.sqrt(HALF)
    pool_scale = 1.0 / math.sqrt(block_len)
    reorder(rows_ref, in_ref, pieces, blocks, True)
    arrived = []
    for j in range(blocks):
        s = rows_ref[j * pieces + 32 : j * pieces + 48, 512:640].astype(F32)[:, :HALF]
        arrived.append(from_head_rows(s[0:2] + s[2:4] + s[4:6]))
    sortq_grad = jnp.concatenate(arrived, axis=0)
    row_grad = dot(
        sortq_grad, block_diagonal(w_ref), ((1,), (1,)), precision=lax.Precision.HIGHEST
    )
    extra_ref[...] = pool_scale * (row_grad + column_ref[...])

    lane = lax.broadcasted_iota(jnp.int32, (LANES, LANES), 1)
    found = jnp.zeros((LANES, LANES), F32)
    for a in range(4):
        s = in_ref[a * LANES : (a + 1) * LANES, 512:640].astype(F32)
        s = s + pltpu.roll(s, LANES - 16, 1) + pltpu.roll(s, LANES - 32, 1)
        s = pltpu.roll(s, (16 * a - SHARE_AT) % LANES, 1)
        found = found + jnp.where((lane >= 16 * a) & (lane < 16 * a + 16), s, 0.0)
    sort_out[...] = found[:, :HALF]

    def step(j, carry):
        at = pl.ds(pl.multiple_of(j * block_len, block_len), block_len)
        here = pl.ds(pl.multiple_of(j * pieces, pieces), pieces)
        kb, vb = k_ref[at, :], v_ref[at, :]
        qs = head_stack(q_ref[at, :], score_scale)
        gs = head_stack(g_ref[at, :], 1.0)
        far = rows_ref[here, 0:512].astype(F32)
        stats = rows_ref[here, 512:640].astype(F32)
        lse = from_rows(stats[0:8, :HALF] + stats[8:16, :HALF] + stats[16:24, :HALF])
        delta = jnp.concatenate([delta_ref[0:1, at], delta_ref[1:2, at]], axis=1)
        scores = dot(kb, qs, ((1,), (1,)))
        probs = jnp.exp(scores - lse)
        low = probs.astype(BF16)
        dprobs = dot(vb, gs, ((1,), (1,)))
        dscores = (probs * (dprobs - delta)).astype(BF16)
        dk = dot(dscores, qs, ((1,), (0,)))
        dk_out[at, :] = (
            dk + dk_far_ref[at, :].astype(F32) + extra_ref[pl.ds(j, 1), :]
        ).astype(BF16)
        dv = dot(low, gs, ((1,), (0,)))
        dv_out[at, :] = (dv + dv_far_ref[at, :].astype(F32)).astype(BF16)
        dq = dot(kb, dscores, ((0,), (0,))) * score_scale
        dq = jnp.concatenate(
            [
                dq[:HALF, :block_len] + far[:, :block_len],
                dq[HALF:, block_len:] + far[:, block_len:],
            ],
            axis=0,
        )
        dq_out[at, :] = dq.T.astype(BF16)
        return carry

    lax.fori_loop(0, blocks, step, 0)


def whole(memory_space=pltpu.VMEM):
    return pl.BlockSpec(memory_space=memory_space)


def call(kernel, outs, inputs, scratch=(), specs=None, flops=1 << 28):
    shapes = [jax.ShapeDtypeStruct(shape, dtype) for shape, dtype in outs]
    size = sum(math.prod(s.shape) * s.dtype.itemsize for s in shapes)
    size += sum(x.size * x.dtype.itemsize for x in inputs)
    return pl.pallas_call(
        kernel,
        out_shape=shapes,
        in_specs=specs or [whole()] * len(inputs),
        out_specs=[whole()] * len(shapes),
        scratch_shapes=list(scratch),
        compiler_params=pltpu.CompilerParams(vmem_limit_bytes=VMEM_LIMIT),
        cost_estimate=pl.CostEstimate(flops=flops, bytes_accessed=size, transcendentals=1 << 20),
    )(*inputs)


def exchange(x):
    return lax.all_to_all(x, "seq", split_axis=0, concat_axis=0, tiled=True)


def per_device(queries, keys, values, delta, dout, partner, sort_weight):
    tokens = queries.shape[0]
    rows = lax.axis_size("seq") * partner.shape[0]
    sent, summary = call(
        pack_kernel,
        [((rows, 1152), BF16), ((8, LANES), F32)],
        [partner, queries, keys, dout, delta],
        scratch=[pltpu.VMEM((rows, 1152), BF16)],
        specs=[whole(pltpu.SMEM)] + [whole()] * 4,
    )
    spread = exchange(sent)
    (moved,) = call(forward_kernel, [((rows, 1152), BF16)], [spread])
    arrived = exchange(moved)
    back, dk_far, dv_far, column = call(
        far_kernel,
        [
            ((rows, 640), BF16),
            ((tokens, LANES), BF16),
            ((tokens, LANES), BF16),
            ((8, LANES), F32),
        ],
        [arrived, keys, values, summary, sort_weight],
        scratch=[
            pltpu.VMEM((rows, 1152), BF16),
            pltpu.VMEM((rows, 640), BF16),
            pltpu.VMEM((8, LANES), F32),
            pltpu.VMEM((8, LANES), F32),
        ],
    )
    spread_back = exchange(back)
    (moved_back,) = call(
        backward_kernel, [((rows, 640), BF16)], [spread[:, 1024:1152], spread_back]
    )
    arrived_back = exchange(moved_back)
    d_queries, d_keys, d_values, d_sort = call(
        self_kernel,
        [((tokens, LANES), BF16)] * 3 + [((LANES, HALF), F32)],
        [
            arrived_back,
            queries,
            keys,
            values,
            dout,
            delta,
            sort_weight,
            dk_far,
            dv_far,
            column,
        ],
        scratch=[pltpu.VMEM((rows, 640), BF16), pltpu.VMEM((8, LANES), F32)],
    )
    return d_queries, d_keys, d_values, d_sort.reshape(sort_weight.shape)


def solution(mesh):
    in_specs = (
        P("seq", "head"),
        P("seq", "head"),
        P("seq", "head"),
        P("head", "seq"),
        P("seq", "head"),
        P("seq"),
        P("head", None, None),
    )
    out_specs = (P("seq", "head"), P("seq", "head"), P("seq", "head"), P("head", None, None))
    return jax.shard_map(
        per_device, mesh=mesh, in_specs=in_specs, out_specs=out_specs, check_vma=False
    )
```

```python
import functools
import math

import jax
import jax.numpy as jnp
from jax import lax
from jax.experimental import pallas as pl
from jax.experimental.pallas import tpu as pltpu
from jax.sharding import PartitionSpec as P

F32 = jnp.float32
BF16 = jnp.bfloat16
LANES = 128
HALF = 64
SHARE_AT = 64
VMEM_LIMIT = 48 * 1024 * 1024


def dot(a, b, dims, **kw):
    return lax.dot_general(a, b, (dims, ((), ())), preferred_element_type=F32, **kw)


def head_stack(x, scale):
    lane = lax.broadcasted_iota(jnp.int32, x.shape, 1)
    x32 = x.astype(F32) * scale
    first = jnp.where(lane < HALF, x32, 0.0)
    second = jnp.where(lane < HALF, 0.0, x32)
    return jnp.concatenate([first, second], axis=0).astype(BF16)


def split3(x):
    high = x.astype(BF16).astype(F32)
    rest = x - high
    mid = rest.astype(BF16).astype(F32)
    return high, mid, (rest - mid).astype(BF16).astype(F32)


def to_rows(v):
    return jnp.concatenate([v[:, i * HALF : (i + 1) * HALF] for i in range(8)], axis=0)


def from_rows(x):
    return jnp.concatenate([x[i : i + 1, :] for i in range(8)], axis=1)


def head_rows(v):
    return jnp.concatenate([v[:, :HALF], v[:, HALF:]], axis=0)


def from_head_rows(x):
    return jnp.concatenate([x[0:1, :], x[1:2, :]], axis=1)


def block_diagonal(w_ref):
    zero = jnp.zeros((HALF, HALF), F32)
    top = jnp.concatenate([w_ref[0], zero], axis=1)
    bottom = jnp.concatenate([zero, w_ref[1]], axis=1)
    return jnp.concatenate([top, bottom], axis=0)


def head_sums(x):
    lane = lax.broadcasted_iota(jnp.int32, x.shape, 1)
    first = jnp.sum(jnp.where(lane < HALF, x, 0.0), axis=1, keepdims=True)
    second = jnp.sum(jnp.where(lane < HALF, 0.0, x), axis=1, keepdims=True)
    return jnp.where(lane < HALF, first, second)


def reorder(rows_ref, source_ref, pieces, blocks, to_blocks):
    total = pieces * blocks
    out_row = lax.broadcasted_iota(jnp.int32, (total, total), 0)
    in_row = lax.broadcasted_iota(jnp.int32, (total, total), 1)
    if to_blocks:
        wanted = (out_row & (pieces - 1)) * blocks + (out_row >> 6)
    else:
        wanted = (out_row & (blocks - 1)) * pieces + (out_row >> 3)
    pick = jnp.where(wanted == in_row, 1.0, 0.0).astype(BF16)
    width = source_ref.shape[1]
    for start in range(0, width, 256):
        stop = min(width, start + 256)
        rows_ref[:, start:stop] = dot(pick, source_ref[:, start:stop], ((1,), (0,))).astype(BF16)


def fold(block, pieces):
    return jnp.concatenate(
        [block[c * pieces : (c + 1) * pieces, :] for c in range(block.shape[0] // pieces)], axis=1
    )


def unfold(rows):
    return jnp.concatenate(
        [rows[:, c * LANES : (c + 1) * LANES] for c in range(rows.shape[1] // LANES)], axis=0
    )


def pack_kernel(partner_ref, q_ref, k_ref, g_ref, delta_ref, out_ref, summary_ref, rows_ref):
    blocks, pieces, block_len = 8, 64, 256
    score_scale = 1.0 / math.sqrt(HALF)
    pool_scale = 1.0 / math.sqrt(block_len)

    def step(j, carry):
        at = pl.ds(pl.multiple_of(j * block_len, block_len), block_len)
        qb, kb, gb = q_ref[at, :], k_ref[at, :], g_ref[at, :]
        scores = dot(kb, head_stack(qb, score_scale), ((1,), (1,)))
        top = jnp.max(scores, axis=0, keepdims=True)
        lse = top + jnp.log(jnp.sum(jnp.exp(scores - top), axis=0, keepdims=True))
        summary = jnp.sum(kb.astype(F32), axis=0, keepdims=True) * pool_scale
        summary_ref[pl.ds(j, 1), :] = summary
        delta = jnp.concatenate([delta_ref[0:1, at], delta_ref[1:2, at]], axis=1)
        stats = jnp.concatenate([to_rows(lse), to_rows(delta)], axis=0)
        parts = jnp.concatenate(split3(stats), axis=0)
        summary_parts = jnp.concatenate(
            list(split3(head_rows(summary))) + [jnp.zeros((10, HALF), F32)], axis=0
        )
        left = jnp.concatenate([parts, summary_parts], axis=0)
        lane = lax.broadcasted_iota(jnp.int32, (pieces, HALF), 1)
        place = partner_ref[j]
        right = jnp.where(
            lane == 0,
            (place >> 3).astype(F32),
            jnp.where(lane == 1, (place & 7).astype(F32), 0.0),
        )
        to = pl.ds(pl.multiple_of(j * pieces, pieces), pieces)
        rows_ref[to, 0:512] = fold(qb, pieces)
        rows_ref[to, 512:1024] = fold(gb, pieces)
        rows_ref[to, 1024:1152] = jnp.concatenate([left, right], axis=1).astype(BF16)
        return carry

    lax.fori_loop(0, blocks, step, 0, unroll=True)
    reorder(out_ref, rows_ref, pieces, blocks, False)


def partner_pick(tags):
    rows = tags.shape[0]
    place = tags[:, HALF : HALF + 1].astype(F32) * 8.0 + tags[:, HALF + 1 : HALF + 2].astype(F32)
    lane = lax.broadcasted_iota(jnp.int32, (rows, rows), 1).astype(F32)
    return jnp.where(lane == place, 1.0, 0.0).astype(BF16)


def forward_kernel(in_ref, out_ref):
    pick = partner_pick(in_ref[:, 1024:1152])
    for start in range(0, 1152, 256):
        stop = min(1152, start + 256)
        out_ref[:, start:stop] = dot(pick, in_ref[:, start:stop], ((0,), (0,))).astype(BF16)


def backward_kernel(tags_ref, in_ref, out_ref):
    pick = partner_pick(tags_ref[...])
    for start in (0, 256):
        out_ref[:, start : start + 256] = dot(
            pick, in_ref[:, start : start + 256], ((1,), (0,))
        ).astype(BF16)
    tail = in_ref[:, 512:640]
    moved = dot(pick, tail, ((1,), (0,)))
    rows = tail.shape[0]
    total = jnp.sum(tail.astype(F32).reshape(rows // 8, 8, LANES), axis=0)
    lane8 = lax.broadcasted_iota(jnp.int32, (8, LANES), 1)
    total = total + pltpu.roll(total, LANES - 16, 1) + pltpu.roll(total, LANES - 32, 1)
    total = jnp.where((lane8 >= SHARE_AT) & (lane8 < SHARE_AT + 16), total, 0.0)
    high, mid, low = split3(total)
    share = high + pltpu.roll(mid, 16, 1) + pltpu.roll(low, 32, 1)
    share = jnp.broadcast_to(share[None], (rows // 8, 8, LANES)).reshape(rows, LANES)
    lane = lax.broadcasted_iota(jnp.int32, (rows, LANES), 1)
    out_ref[:, 512:640] = jnp.where(lane < SHARE_AT, moved, share).astype(BF16)


def far_kernel(
    in_ref,
    k_ref,
    v_ref,
    summary_ref,
    w_ref,
    out_ref,
    dk_ref,
    dv_ref,
    column_ref,
    rows_ref,
    back_ref,
    gate_ref,
    grad_ref,
):
    blocks, pieces, block_len = 8, 64, 256
    score_scale = 1.0 / math.sqrt(HALF)
    reorder(rows_ref, in_ref, pieces, blocks, True)
    arrived = []
    for j in range(blocks):
        s = rows_ref[j * pieces + 48 : j * pieces + 64, 1024:1152].astype(F32)[:, :HALF]
        arrived.append(from_head_rows(s[0:2] + s[2:4] + s[4:6]))
    summary_in = jnp.concatenate(arrived, axis=0)
    summary = summary_ref[...]
    sortq = dot(summary_in, block_diagonal(w_ref), ((1,), (0,)), precision=lax.Precision.HIGHEST)
    gates = jax.nn.sigmoid(score_scale * head_sums(sortq * summary))
    gate_ref[...] = gates

    def step(j, carry):
        at = pl.ds(pl.multiple_of(j * block_len, block_len), block_len)
        here = pl.ds(pl.multiple_of(j * pieces, pieces), pieces)
        kb, vb = k_ref[at, :], v_ref[at, :]
        qs = head_stack(unfold(rows_ref[here, 0:512]), score_scale)
        gs = head_stack(unfold(rows_ref[here, 512:1024]), 1.0)
        stats = rows_ref[here, 1024:1152].astype(F32)
        joined = stats[0:16, :HALF] + stats[16:32, :HALF] + stats[32:48, :HALF]
        own_lse = from_rows(joined[0:8])
        delta = from_rows(joined[8:16])
        gate = gate_ref[pl.ds(j, 1), :]
        gate_row = jnp.concatenate(
            [
                jnp.broadcast_to(gate[:, 0:1], (1, block_len)),
                jnp.broadcast_to(gate[:, HALF : HALF + 1], (1, block_len)),
            ],
            axis=1,
        )
        scores = dot(kb, qs, ((1,), (1,)))
        top = jnp.maximum(own_lse, jnp.max(scores, axis=0, keepdims=True))
        weights = jnp.exp(scores - top)
        total = jnp.exp(own_lse - top) + jnp.sum(weights, axis=0, keepdims=True)
        probs = weights * (1.0 / total)
        lse = top + jnp.log(total)
        low = probs.astype(BF16)
        dprobs = dot(vb, gs, ((1,), (1,)))
        gate_terms = jnp.sum(low.astype(F32) * dprobs, axis=0, keepdims=True)
        first = jnp.sum(gate_terms[:, :block_len], axis=1, keepdims=True)
        second = jnp.sum(gate_terms[:, block_len:], axis=1, keepdims=True)
        lane = lax.broadcasted_iota(jnp.int32, (1, LANES), 1)
        grad_ref[pl.ds(j, 1), :] = jnp.where(lane < HALF, first, second)
        dscores = (probs * (gate_row * dprobs - delta)).astype(BF16)
        dk_ref[at, :] = dot(dscores, qs, ((1,), (0,))).astype(BF16)
        dv_ref[at, :] = (dot(low, gs, ((1,), (0,))) * gate).astype(BF16)
        dq = dot(kb, dscores, ((0,), (0,))) * score_scale
        dq = jnp.concatenate([dq[:HALF, :block_len], dq[HALF:, block_len:]], axis=1)
        back_ref[here, 0:512] = dq.astype(BF16)
        parts = jnp.concatenate(
            list(split3(to_rows(lse))) + [jnp.zeros((pieces - 24, HALF), F32)], axis=0
        )
        back_ref[here, 512:640] = jnp.concatenate(
            [parts, jnp.zeros((pieces, HALF), F32)], axis=1
        ).astype(BF16)
        return carry

    lax.fori_loop(0, blocks, step, 0, unroll=True)
    logit_grad = grad_ref[...] * gates * (1.0 - gates)
    sortq_grad = score_scale * logit_grad * summary
    column_ref[...] = score_scale * logit_grad * sortq
    for j in range(blocks):
        parts = jnp.concatenate(
            list(split3(head_rows(sortq_grad[j : j + 1, :]))) + [jnp.zeros((10, HALF), F32)],
            axis=0,
        )
        back_ref[j * pieces + 32 : j * pieces + 48, 512:640] = jnp.concatenate(
            [parts, jnp.zeros((16, HALF), F32)], axis=1
        ).astype(BF16)
    reorder(out_ref, back_ref, pieces, blocks, False)
    outer = dot(summary_in, sortq_grad, ((0,), (0,)), precision=lax.Precision.HIGHEST)
    lane = lax.broadcasted_iota(jnp.int32, (LANES, LANES), 1)
    row = lax.broadcasted_iota(jnp.int32, (LANES, LANES), 0)
    outer = jnp.where(row < HALF, outer, pltpu.roll(outer, HALF, 1))
    inside = (lane >= SHARE_AT) & (lane < SHARE_AT + 16)
    for a in range(4):
        part = jnp.where(inside, pltpu.roll(outer, (SHARE_AT - 16 * a) % LANES, 1), 0.0)
        high, mid, low = split3(part)
        share = high + pltpu.roll(mid, 16, 1) + pltpu.roll(low, 32, 1)
        rows = slice(a * LANES, (a + 1) * LANES)
        out_ref[rows, 512:640] = (out_ref[rows, 512:640].astype(F32) + share).astype(BF16)


def self_kernel(
    in_ref,
    q_ref,
    k_ref,
    v_ref,
    g_ref,
    delta_ref,
    w_ref,
    dk_far_ref,
    dv_far_ref,
    column_ref,
    dq_out,
    dk_out,
    dv_out,
    sort_out,
    rows_ref,
    extra_ref,
):
    blocks, pieces, block_len = 8, 64, 256
    score_scale = 1.0 / math.sqrt(HALF)
    pool_scale = 1.0 / math.sqrt(block_len)
    reorder(rows_ref, in_ref, pieces, blocks, True)
    arrived = []
    for j in range(blocks):
        s = rows_ref[j * pieces + 32 : j * pieces + 48, 512:640].astype(F32)[:, :HALF]
        arrived.append(from_head_rows(s[0:2] + s[2:4] + s[4:6]))
    sortq_grad = jnp.concatenate(arrived, axis=0)
    row_grad = dot(
        sortq_grad, block_diagonal(w_ref), ((1,), (1,)), precision=lax.Precision.HIGHEST
    )
    extra_ref[...] = pool_scale * (row_grad + column_ref[...])

    lane = lax.broadcasted_iota(jnp.int32, (LANES, LANES), 1)
    found = jnp.zeros((LANES, LANES), F32)
    for a in range(4):
        s = in_ref[a * LANES : (a + 1) * LANES, 512:640].astype(F32)
        s = s + pltpu.roll(s, LANES - 16, 1) + pltpu.roll(s, LANES - 32, 1)
        s = pltpu.roll(s, (16 * a - SHARE_AT) % LANES, 1)
        found = found + jnp.where((lane >= 16 * a) & (lane < 16 * a + 16), s, 0.0)
    sort_out[...] = found[:, :HALF]

    def step(j, carry):
        at = pl.ds(pl.multiple_of(j * block_len, block_len), block_len)
        here = pl.ds(pl.multiple_of(j * pieces, pieces), pieces)
        kb, vb = k_ref[at, :], v_ref[at, :]
        qs = head_stack(q_ref[at, :], score_scale)
        gs = head_stack(g_ref[at, :], 1.0)
        far = rows_ref[here, 0:512].astype(F32)
        stats = rows_ref[here, 512:640].astype(F32)
        lse = from_rows(stats[0:8, :HALF] + stats[8:16, :HALF] + stats[16:24, :HALF])
        delta = jnp.concatenate([delta_ref[0:1, at], delta_ref[1:2, at]], axis=1)
        scores = dot(kb, qs, ((1,), (1,)))
        probs = jnp.exp(scores - lse)
        low = probs.astype(BF16)
        dprobs = dot(vb, gs, ((1,), (1,)))
        dscores = (probs * (dprobs - delta)).astype(BF16)
        dk = dot(dscores, qs, ((1,), (0,)))
        dk_out[at, :] = (
            dk + dk_far_ref[at, :].astype(F32) + extra_ref[pl.ds(j, 1), :]
        ).astype(BF16)
        dv = dot(low, gs, ((1,), (0,)))
        dv_out[at, :] = (dv + dv_far_ref[at, :].astype(F32)).astype(BF16)
        dq = dot(kb, dscores, ((0,), (0,))) * score_scale
        dq = jnp.concatenate(
            [
                dq[:HALF, :block_len] + far[:, :block_len],
                dq[HALF:, block_len:] + far[:, block_len:],
            ],
            axis=0,
        )
        dq_out[at, :] = dq.T.astype(BF16)
        return carry

    lax.fori_loop(0, blocks, step, 0, unroll=True)


def whole(memory_space=pltpu.VMEM):
    return pl.BlockSpec(memory_space=memory_space)


def call(kernel, outs, inputs, scratch=(), specs=None, flops=1 << 28):
    shapes = [jax.ShapeDtypeStruct(shape, dtype) for shape, dtype in outs]
    size = sum(math.prod(s.shape) * s.dtype.itemsize for s in shapes)
    size += sum(x.size * x.dtype.itemsize for x in inputs)
    return pl.pallas_call(
        kernel,
        out_shape=shapes,
        in_specs=specs or [whole()] * len(inputs),
        out_specs=[whole()] * len(shapes),
        scratch_shapes=list(scratch),
        compiler_params=pltpu.CompilerParams(vmem_limit_bytes=VMEM_LIMIT),
        cost_estimate=pl.CostEstimate(flops=flops, bytes_accessed=size, transcendentals=1 << 20),
    )(*inputs)


def exchange(x):
    return lax.all_to_all(x, "seq", split_axis=0, concat_axis=0, tiled=True)


def per_device(queries, keys, values, delta, dout, partner, sort_weight):
    tokens = queries.shape[0]
    rows = lax.axis_size("seq") * partner.shape[0]
    sent, summary = call(
        pack_kernel,
        [((rows, 1152), BF16), ((8, LANES), F32)],
        [partner, queries, keys, dout, delta],
        scratch=[pltpu.VMEM((rows, 1152), BF16)],
        specs=[whole(pltpu.SMEM)] + [whole()] * 4,
    )
    spread = exchange(sent)
    (moved,) = call(forward_kernel, [((rows, 1152), BF16)], [spread])
    arrived = exchange(moved)
    back, dk_far, dv_far, column = call(
        far_kernel,
        [
            ((rows, 640), BF16),
            ((tokens, LANES), BF16),
            ((tokens, LANES), BF16),
            ((8, LANES), F32),
        ],
        [arrived, keys, values, summary, sort_weight],
        scratch=[
            pltpu.VMEM((rows, 1152), BF16),
            pltpu.VMEM((rows, 640), BF16),
            pltpu.VMEM((8, LANES), F32),
            pltpu.VMEM((8, LANES), F32),
        ],
    )
    spread_back = exchange(back)
    (moved_back,) = call(
        backward_kernel, [((rows, 640), BF16)], [spread[:, 1024:1152], spread_back]
    )
    arrived_back = exchange(moved_back)
    d_queries, d_keys, d_values, d_sort = call(
        self_kernel,
        [((tokens, LANES), BF16)] * 3 + [((LANES, HALF), F32)],
        [
            arrived_back,
            queries,
            keys,
            values,
            dout,
            delta,
            sort_weight,
            dk_far,
            dv_far,
            column,
        ],
        scratch=[pltpu.VMEM((rows, 640), BF16), pltpu.VMEM((8, LANES), F32)],
    )
    return d_queries, d_keys, d_values, d_sort.reshape(sort_weight.shape)


def solution(mesh):
    in_specs = (
        P("seq", "head"),
        P("seq", "head"),
        P("seq", "head"),
        P("head", "seq"),
        P("seq", "head"),
        P("seq"),
        P("head", None, None),
    )
    out_specs = (P("seq", "head"), P("seq", "head"), P("seq", "head"), P("head", None, None))
    return jax.shard_map(
        per_device, mesh=mesh, in_specs=in_specs, out_specs=out_specs, check_vma=False
    )
```

```python
import functools
import math

import jax
import jax.numpy as jnp
from jax import lax
from jax.experimental import pallas as pl
from jax.experimental.pallas import tpu as pltpu
from jax.sharding import PartitionSpec as P

F32 = jnp.float32
BF16 = jnp.bfloat16
LANES = 128
HALF = 64
SHARE_AT = 64
VMEM_LIMIT = 48 * 1024 * 1024
WHOLE_LIMIT = 62240000


def dot(a, b, dims, **kw):
    return lax.dot_general(a, b, (dims, ((), ())), preferred_element_type=F32, **kw)


def head_stack(x, scale):
    lane = lax.broadcasted_iota(jnp.int32, x.shape, 1)
    x32 = x.astype(F32) * scale
    first = jnp.where(lane < HALF, x32, 0.0)
    second = jnp.where(lane < HALF, 0.0, x32)
    return jnp.concatenate([first, second], axis=0).astype(BF16)


def split3(x):
    high = x.astype(BF16).astype(F32)
    rest = x - high
    mid = rest.astype(BF16).astype(F32)
    return high, mid, (rest - mid).astype(BF16).astype(F32)


def to_rows(v):
    return jnp.concatenate([v[:, i * HALF : (i + 1) * HALF] for i in range(8)], axis=0)


def from_rows(x):
    return jnp.concatenate([x[i : i + 1, :] for i in range(8)], axis=1)


def head_rows(v):
    return jnp.concatenate([v[:, :HALF], v[:, HALF:]], axis=0)


def from_head_rows(x):
    return jnp.concatenate([x[0:1, :], x[1:2, :]], axis=1)


def block_diagonal(w_ref):
    zero = jnp.zeros((HALF, HALF), F32)
    top = jnp.concatenate([w_ref[0], zero], axis=1)
    bottom = jnp.concatenate([zero, w_ref[1]], axis=1)
    return jnp.concatenate([top, bottom], axis=0)


def head_sums(x):
    lane = lax.broadcasted_iota(jnp.int32, x.shape, 1)
    first = jnp.sum(jnp.where(lane < HALF, x, 0.0), axis=1, keepdims=True)
    second = jnp.sum(jnp.where(lane < HALF, 0.0, x), axis=1, keepdims=True)
    return jnp.where(lane < HALF, first, second)


def pick_rows(total, inner):
    out_row = lax.broadcasted_iota(jnp.int32, (total, total), 0)
    in_row = lax.broadcasted_iota(jnp.int32, (total, total), 1)
    outer = total // inner
    wanted = (out_row & (outer - 1)) * inner + (out_row >> int(math.log2(outer)))
    return jnp.where(wanted == in_row, 1.0, 0.0).astype(BF16)


def chunks(width):
    return [(start, min(width, start + 256)) for start in range(0, width, 256)]


def to_blocks(rows_ref, source_ref, pieces, blocks):
    half = pieces // 2
    total = half * blocks
    pick = pick_rows(total, blocks)
    for start, stop in chunks(source_ref.shape[1]):
        for h in range(2):
            moved = dot(pick, source_ref[h * total : (h + 1) * total, start:stop], ((1,), (0,)))
            moved = moved.astype(BF16)
            for j in range(blocks):
                at = j * pieces + h * half
                rows_ref[at : at + half, start:stop] = moved[j * half : (j + 1) * half]


def to_pieces(out_ref, rows_ref, pieces, blocks, spans):
    half = pieces // 2
    total = half * blocks
    pick = pick_rows(total, half)
    for start, stop in spans:
        for h in range(2):
            part = [
                rows_ref[j * pieces + h * half : j * pieces + (h + 1) * half, start:stop]
                for j in range(blocks)
            ]
            moved = dot(pick, jnp.concatenate(part, axis=0), ((1,), (0,)))
            out_ref[h * total : (h + 1) * total, start:stop] = moved.astype(BF16)


def fold(block, pieces):
    return jnp.concatenate(
        [block[c * pieces : (c + 1) * pieces, :] for c in range(block.shape[0] // pieces)], axis=1
    )


def unfold(rows):
    return jnp.concatenate(
        [rows[:, c * LANES : (c + 1) * LANES] for c in range(rows.shape[1] // LANES)], axis=0
    )


def pack_kernel(
    partner_hbm,
    q_hbm,
    k_hbm,
    g_hbm,
    delta_hbm,
    out_ref,
    summary_ref,
    rows_ref,
    partner_ref,
    q_ref,
    k_ref,
    g_ref,
    delta_ref,
    sems,
    small_sems,
):
    blocks, pieces, block_len = 8, 64, 256
    score_scale = 1.0 / math.sqrt(HALF)
    pool_scale = 1.0 / math.sqrt(block_len)
    copies = []
    for half in range(2):
        at = pl.ds(half * blocks // 2 * block_len, blocks // 2 * block_len)
        pairs = ((k_hbm, k_ref), (q_hbm, q_ref), (g_hbm, g_ref))
        copies.append(
            [
                pltpu.make_async_copy(there.at[at], here.at[at], sems.at[half, i])
                for i, (there, here) in enumerate(pairs)
            ]
        )
    copies[0] += [
        pltpu.make_async_copy(delta_hbm, delta_ref, small_sems.at[0]),
        pltpu.make_async_copy(partner_hbm, partner_ref, small_sems.at[1]),
    ]
    for copy in copies[0] + copies[1]:
        copy.start()

    for j in range(blocks):
        if j % (blocks // 2) == 0:
            for copy in copies[j // (blocks // 2)]:
                copy.wait()
        at = slice(j * block_len, (j + 1) * block_len)
        qb, kb, gb = q_ref[at, :], k_ref[at, :], g_ref[at, :]
        scores = dot(kb, head_stack(qb, score_scale), ((1,), (1,)))
        top = jnp.max(scores, axis=0, keepdims=True)
        lse = top + jnp.log(jnp.sum(jnp.exp(scores - top), axis=0, keepdims=True))
        summary = jnp.sum(kb.astype(F32), axis=0, keepdims=True) * pool_scale
        summary_ref[j : j + 1, :] = summary
        delta = jnp.concatenate([delta_ref[0:1, at], delta_ref[1:2, at]], axis=1)
        stats = jnp.concatenate([to_rows(lse), to_rows(delta)], axis=0)
        parts = jnp.concatenate(split3(stats), axis=0)
        summary_parts = jnp.concatenate(
            list(split3(head_rows(summary))) + [jnp.zeros((10, HALF), F32)], axis=0
        )
        left = jnp.concatenate([parts, summary_parts], axis=0)
        lane = lax.broadcasted_iota(jnp.int32, (pieces, HALF), 1)
        place = partner_ref[j]
        right = jnp.where(
            lane == 0,
            (place >> 3).astype(F32),
            jnp.where(lane == 1, (place & 7).astype(F32), 0.0),
        )
        to = slice(j * pieces, (j + 1) * pieces)
        rows_ref[to, 0:512] = fold(qb, pieces)
        rows_ref[to, 512:1024] = fold(gb, pieces)
        rows_ref[to, 1024:1152] = jnp.concatenate([left, right], axis=1).astype(BF16)

    to_pieces(out_ref, rows_ref, pieces, blocks, chunks(1152))


def partner_pick(place):
    rows = place.shape[1]
    row = lax.broadcasted_iota(jnp.int32, (rows, rows), 0).astype(F32)
    return jnp.where(row == place, 1.0, 0.0).astype(BF16)


def forward_kernel(in_ref, out_ref, place_ref):
    tags = in_ref[:, 1024:1152].astype(F32).T
    place = tags[HALF : HALF + 1, :] * 8.0 + tags[HALF + 1 : HALF + 2, :]
    place_ref[...] = place
    pick = partner_pick(place)
    for start in range(0, 1152, 256):
        stop = min(1152, start + 256)
        out_ref[:, start:stop] = dot(pick, in_ref[:, start:stop], ((1,), (0,))).astype(BF16)


def backward_kernel(place_ref, in_ref, out_ref):
    pick = partner_pick(place_ref[...])
    for start in (0, 256):
        out_ref[:, start : start + 256] = dot(
            pick, in_ref[:, start : start + 256], ((0,), (0,))
        ).astype(BF16)
    tail = in_ref[:, 512:640]
    moved = dot(pick, tail, ((0,), (0,)))
    rows = tail.shape[0]
    total = jnp.sum(tail.astype(F32).reshape(rows // 8, 8, LANES), axis=0)
    lane8 = lax.broadcasted_iota(jnp.int32, (8, LANES), 1)
    total = total + pltpu.roll(total, LANES - 16, 1) + pltpu.roll(total, LANES - 32, 1)
    total = jnp.where((lane8 >= SHARE_AT) & (lane8 < SHARE_AT + 16), total, 0.0)
    high, mid, low = split3(total)
    share = high + pltpu.roll(mid, 16, 1) + pltpu.roll(low, 32, 1)
    share = jnp.broadcast_to(share[None], (rows // 8, 8, LANES)).reshape(rows, LANES)
    lane = lax.broadcasted_iota(jnp.int32, (rows, LANES), 1)
    out_ref[:, 512:640] = jnp.where(lane < SHARE_AT, moved, share).astype(BF16)


def far_kernel(
    in_ref,
    k_ref,
    v_ref,
    summary_ref,
    w_ref,
    out_ref,
    dk_ref,
    dv_ref,
    column_ref,
    rows_ref,
    back_ref,
    gate_ref,
    grad_ref,
):
    blocks, pieces, block_len = 8, 64, 256
    score_scale = 1.0 / math.sqrt(HALF)
    to_blocks(rows_ref, in_ref, pieces, blocks)
    arrived = []
    for j in range(blocks):
        s = rows_ref[j * pieces + 48 : j * pieces + 64, 1024:1152].astype(F32)[:, :HALF]
        arrived.append(from_head_rows(s[0:2] + s[2:4] + s[4:6]))
    summary_in = jnp.concatenate(arrived, axis=0)
    summary = summary_ref[...]
    sortq = dot(summary_in, block_diagonal(w_ref), ((1,), (0,)), precision=lax.Precision.HIGHEST)
    gates = jax.nn.sigmoid(score_scale * head_sums(sortq * summary))
    gate_ref[...] = gates

    def step(j, carry):
        at = pl.ds(pl.multiple_of(j * block_len, block_len), block_len)
        here = pl.ds(pl.multiple_of(j * pieces, pieces), pieces)
        kb, vb = k_ref[at, :], v_ref[at, :]
        qs = head_stack(unfold(rows_ref[here, 0:512]), score_scale)
        gs = head_stack(unfold(rows_ref[here, 512:1024]), 1.0)
        stats = rows_ref[here, 1024:1152].astype(F32)
        joined = stats[0:16, :HALF] + stats[16:32, :HALF] + stats[32:48, :HALF]
        own_lse = from_rows(joined[0:8])
        delta = from_rows(joined[8:16])
        gate = gate_ref[pl.ds(j, 1), :]
        gate_row = jnp.concatenate(
            [
                jnp.broadcast_to(gate[:, 0:1], (1, block_len)),
                jnp.broadcast_to(gate[:, HALF : HALF + 1], (1, block_len)),
            ],
            axis=1,
        )
        scores = dot(kb, qs, ((1,), (1,)))
        top = jnp.maximum(own_lse, jnp.max(scores, axis=0, keepdims=True))
        weights = jnp.exp(scores - top)
        total = jnp.exp(own_lse - top) + jnp.sum(weights, axis=0, keepdims=True)
        probs = weights * (1.0 / total)
        lse = top + jnp.log(total)
        low = probs.astype(BF16)
        dprobs = dot(vb, gs, ((1,), (1,)))
        gate_terms = jnp.sum(low.astype(F32) * dprobs, axis=0, keepdims=True)
        first = jnp.sum(gate_terms[:, :block_len], axis=1, keepdims=True)
        second = jnp.sum(gate_terms[:, block_len:], axis=1, keepdims=True)
        lane = lax.broadcasted_iota(jnp.int32, (1, LANES), 1)
        grad_ref[pl.ds(j, 1), :] = jnp.where(lane < HALF, first, second)
        dscores = (probs * (gate_row * dprobs - delta)).astype(BF16)
        dk_ref[at, :] = dot(dscores, qs, ((1,), (0,))).astype(BF16)
        dv_ref[at, :] = (dot(low, gs, ((1,), (0,))) * gate).astype(BF16)
        dq = dot(kb, dscores, ((0,), (0,))) * score_scale
        dq = jnp.concatenate([dq[:HALF, :block_len], dq[HALF:, block_len:]], axis=1)
        back_ref[here, 0:512] = dq.astype(BF16)
        parts = jnp.concatenate(
            list(split3(to_rows(lse))) + [jnp.zeros((pieces - 24, HALF), F32)], axis=0
        )
        back_ref[here, 512:640] = jnp.concatenate(
            [parts, jnp.zeros((pieces, HALF), F32)], axis=1
        ).astype(BF16)
        return carry

    lax.fori_loop(0, blocks, step, 0, unroll=True)
    logit_grad = grad_ref[...] * gates * (1.0 - gates)
    sortq_grad = score_scale * logit_grad * summary
    column_ref[...] = score_scale * logit_grad * sortq
    for j in range(blocks):
        parts = jnp.concatenate(
            list(split3(head_rows(sortq_grad[j : j + 1, :]))) + [jnp.zeros((10, HALF), F32)],
            axis=0,
        )
        back_ref[j * pieces + 32 : j * pieces + 48, 512:640] = jnp.concatenate(
            [parts, jnp.zeros((16, HALF), F32)], axis=1
        ).astype(BF16)
    to_pieces(out_ref, back_ref, pieces, blocks, chunks(640))
    outer = dot(summary_in, sortq_grad, ((0,), (0,)), precision=lax.Precision.HIGHEST)
    lane = lax.broadcasted_iota(jnp.int32, (LANES, LANES), 1)
    row = lax.broadcasted_iota(jnp.int32, (LANES, LANES), 0)
    outer = jnp.where(row < HALF, outer, pltpu.roll(outer, HALF, 1))
    inside = (lane >= SHARE_AT) & (lane < SHARE_AT + 16)
    for a in range(4):
        part = jnp.where(inside, pltpu.roll(outer, (SHARE_AT - 16 * a) % LANES, 1), 0.0)
        high, mid, low = split3(part)
        share = high + pltpu.roll(mid, 16, 1) + pltpu.roll(low, 32, 1)
        rows = slice(a * LANES, (a + 1) * LANES)
        out_ref[rows, 512:640] = (out_ref[rows, 512:640].astype(F32) + share).astype(BF16)


def self_kernel(
    in_ref,
    q_ref,
    k_ref,
    v_ref,
    g_ref,
    delta_ref,
    w_ref,
    dk_far_ref,
    dv_far_ref,
    column_ref,
    dq_hbm,
    dk_hbm,
    dv_hbm,
    sort_out,
    rows_ref,
    dq_out,
    dk_out,
    dv_out,
    sems,
):
    blocks, pieces, block_len = 8, 64, 256
    score_scale = 1.0 / math.sqrt(HALF)
    pool_scale = 1.0 / math.sqrt(block_len)
    to_blocks(rows_ref, in_ref, pieces, blocks)
    arrived = []
    for j in range(blocks):
        s = rows_ref[j * pieces + 32 : j * pieces + 48, 512:640].astype(F32)[:, :HALF]
        arrived.append(from_head_rows(s[0:2] + s[2:4] + s[4:6]))
    sortq_grad = jnp.concatenate(arrived, axis=0)
    row_grad = dot(
        sortq_grad, block_diagonal(w_ref), ((1,), (1,)), precision=lax.Precision.HIGHEST
    )
    extra = pool_scale * (row_grad + column_ref[...])

    lane = lax.broadcasted_iota(jnp.int32, (LANES, LANES), 1)
    found = jnp.zeros((LANES, LANES), F32)
    for a in range(4):
        s = in_ref[a * LANES : (a + 1) * LANES, 512:640].astype(F32)
        s = s + pltpu.roll(s, LANES - 16, 1) + pltpu.roll(s, LANES - 32, 1)
        s = pltpu.roll(s, (16 * a - SHARE_AT) % LANES, 1)
        found = found + jnp.where((lane >= 16 * a) & (lane < 16 * a + 16), s, 0.0)
    sort_out[...] = found[:, :HALF]

    copies = []
    for j in range(blocks):
        at = slice(j * block_len, (j + 1) * block_len)
        here = slice(j * pieces, (j + 1) * pieces)
        kb, vb = k_ref[at, :], v_ref[at, :]
        qs = head_stack(q_ref[at, :], score_scale)
        gs = head_stack(g_ref[at, :], 1.0)
        far = rows_ref[here, 0:512].astype(F32)
        stats = rows_ref[here, 512:640].astype(F32)
        lse = from_rows(stats[0:8, :HALF] + stats[8:16, :HALF] + stats[16:24, :HALF])
        delta = jnp.concatenate([delta_ref[0:1, at], delta_ref[1:2, at]], axis=1)
        scores = dot(kb, qs, ((1,), (1,)))
        probs = jnp.exp(scores - lse)
        low = probs.astype(BF16)
        dprobs = dot(vb, gs, ((1,), (1,)))
        dscores = (probs * (dprobs - delta)).astype(BF16)
        dk = dot(dscores, qs, ((1,), (0,)))
        dk_out[at, :] = (dk + dk_far_ref[at, :].astype(F32) + extra[j : j + 1, :]).astype(BF16)
        dv = dot(low, gs, ((1,), (0,)))
        dv_out[at, :] = (dv + dv_far_ref[at, :].astype(F32)).astype(BF16)
        dq = dot(kb, dscores, ((0,), (0,))) * score_scale
        dq = jnp.concatenate(
            [
                dq[:HALF, :block_len] + far[:, :block_len],
                dq[HALF:, block_len:] + far[:, block_len:],
            ],
            axis=0,
        )
        dq_out[at, :] = dq.T.astype(BF16)
        if j % (blocks // 2) == blocks // 2 - 1:
            half = j // (blocks // 2)
            rows = pl.ds(half * blocks // 2 * block_len, blocks // 2 * block_len)
            pairs = ((dq_out, dq_hbm), (dk_out, dk_hbm), (dv_out, dv_hbm))
            for i, (here_ref, there) in enumerate(pairs):
                copy = pltpu.make_async_copy(here_ref.at[rows], there.at[rows], sems.at[half, i])
                copy.start()
                copies.append(copy)

    for copy in copies:
        copy.wait()


def whole(memory_space=pltpu.VMEM):
    return pl.BlockSpec(memory_space=memory_space)


def call(
    kernel, outs, inputs, scratch=(), in_hbm=False, out_hbm=0, limit=VMEM_LIMIT, flops=1 << 28
):
    shapes = [jax.ShapeDtypeStruct(shape, dtype) for shape, dtype in outs]
    size = sum(math.prod(s.shape) * s.dtype.itemsize for s in shapes)
    size += sum(x.size * x.dtype.itemsize for x in inputs)
    return pl.pallas_call(
        kernel,
        out_shape=shapes,
        in_specs=[whole(pl.ANY if in_hbm else pltpu.VMEM)] * len(inputs),
        out_specs=[whole(pl.ANY)] * out_hbm + [whole()] * (len(shapes) - out_hbm),
        scratch_shapes=list(scratch),
        compiler_params=pltpu.CompilerParams(vmem_limit_bytes=limit),
        cost_estimate=pl.CostEstimate(flops=flops, bytes_accessed=size, transcendentals=1 << 20),
    )(*inputs)


def exchange(x):
    return lax.all_to_all(x, "seq", split_axis=0, concat_axis=0, tiled=True)


def per_device(queries, keys, values, delta, dout, partner, sort_weight):
    tokens = queries.shape[0]
    rows = lax.axis_size("seq") * partner.shape[0]
    blocks = partner.shape[0]
    buffer = pltpu.VMEM((tokens, LANES), BF16)
    sent, summary = call(
        pack_kernel,
        [((rows, 1152), BF16), ((blocks, LANES), F32)],
        [partner, queries, keys, dout, delta],
        scratch=[
            pltpu.VMEM((rows, 1152), BF16),
            pltpu.SMEM((blocks,), jnp.int32),
            buffer,
            buffer,
            buffer,
            pltpu.VMEM(delta.shape, F32),
            pltpu.SemaphoreType.DMA((2, 3)),
            pltpu.SemaphoreType.DMA((2,)),
        ],
        in_hbm=True,
        limit=WHOLE_LIMIT,
    )
    spread = exchange(sent)
    moved, place = call(
        forward_kernel, [((rows, 1152), BF16), ((1, rows), F32)], [spread]
    )
    arrived = exchange(moved)
    back, dk_far, dv_far, column = call(
        far_kernel,
        [
            ((rows, 640), BF16),
            ((tokens, LANES), BF16),
            ((tokens, LANES), BF16),
            ((8, LANES), F32),
        ],
        [arrived, keys, values, summary, sort_weight],
        scratch=[
            pltpu.VMEM((rows, 1152), BF16),
            pltpu.VMEM((rows, 640), BF16),
            pltpu.VMEM((8, LANES), F32),
            pltpu.VMEM((8, LANES), F32),
        ],
    )
    spread_back = exchange(back)
    (moved_back,) = call(backward_kernel, [((rows, 640), BF16)], [place, spread_back])
    arrived_back = exchange(moved_back)
    d_queries, d_keys, d_values, d_sort = call(
        self_kernel,
        [((tokens, LANES), BF16)] * 3 + [((LANES, HALF), F32)],
        [
            arrived_back,
            queries,
            keys,
            values,
            dout,
            delta,
            sort_weight,
            dk_far,
            dv_far,
            column,
        ],
        scratch=[
            pltpu.VMEM((rows, 640), BF16),
            buffer,
            buffer,
            buffer,
            pltpu.SemaphoreType.DMA((2, 3)),
        ],
        out_hbm=3,
    )
    return d_queries, d_keys, d_values, d_sort.reshape(sort_weight.shape)


def solution(mesh):
    in_specs = (
        P("seq", "head"),
        P("seq", "head"),
        P("seq", "head"),
        P("head", "seq"),
        P("seq", "head"),
        P("seq"),
        P("head", None, None),
    )
    out_specs = (P("seq", "head"), P("seq", "head"), P("seq", "head"), P("head", None, None))
    return jax.shard_map(
        per_device, mesh=mesh, in_specs=in_specs, out_specs=out_specs, check_vma=False
    )
```

```python
import functools
import math

import jax
import jax.numpy as jnp
from jax import lax
from jax.experimental import pallas as pl
from jax.experimental.pallas import tpu as pltpu
from jax.sharding import PartitionSpec as P

F32 = jnp.float32
BF16 = jnp.bfloat16
LANES = 128
HALF = 64
QUARTER = 32
SHARE = 16
VMEM_LIMIT = 48 * 1024 * 1024
WHOLE_LIMIT = 62240000


def dot(a, b, dims, **kw):
    return lax.dot_general(a, b, (dims, ((), ())), preferred_element_type=F32, **kw)


def head_stack(x, scale):
    lane = lax.broadcasted_iota(jnp.int32, (1, LANES), 1)
    first = jnp.where(lane < HALF, scale, 0.0).astype(BF16)
    second = jnp.where(lane < HALF, 0.0, scale).astype(BF16)
    return jnp.concatenate([x * first, x * second], axis=0)


def split3(x):
    high = x.astype(BF16).astype(F32)
    rest = x - high
    mid = rest.astype(BF16).astype(F32)
    return high, mid, (rest - mid).astype(BF16).astype(F32)


def to_rows(v):
    return jnp.concatenate([v[:, i * HALF : (i + 1) * HALF] for i in range(8)], axis=0)


def from_rows(x):
    return jnp.concatenate([x[i : i + 1, :] for i in range(8)], axis=1)


def head_rows(v):
    return jnp.concatenate([v[:, :HALF], v[:, HALF:]], axis=0)


def from_head_rows(x):
    return jnp.concatenate([x[0:1, :], x[1:2, :]], axis=1)


def narrow(x):
    return jnp.concatenate([x[:, :QUARTER], x[:, QUARTER:]], axis=0)


def widen(x):
    rows = x.shape[0] // 2
    return jnp.concatenate([x[:rows], x[rows:]], axis=1)


def load_slots(ref, start, stop, step):
    low = ref[:, :, start:stop].astype(F32)
    high = ref[:, :, start + step : stop + step].astype(F32)
    both = jnp.concatenate([low, high], axis=1)
    return both.reshape(both.shape[0] * 8, stop - start)


def load_slot_stats(ref):
    both = ref[:, :, 1024:1152].astype(F32)
    both = jnp.concatenate([both, pltpu.roll(both, HALF, 2)], axis=1)
    return both.reshape(both.shape[0] * 8, LANES)


def store_slots(ref, first, rows, start, stop, step):
    slots = rows.reshape(rows.shape[0] // 8, 8, stop - start)
    at = slice(first, first + slots.shape[0])
    ref[at, :, start:stop] = slots[:, :4].astype(BF16)
    ref[at, :, start + step : stop + step] = slots[:, 4:].astype(BF16)


def store_slot_stats(ref, first, rows):
    slots = rows.reshape(rows.shape[0] // 8, 8, LANES)
    lane = lax.broadcasted_iota(jnp.int32, (slots.shape[0], 4, LANES), 2)
    both = jnp.where(lane < HALF, slots[:, :4], pltpu.roll(slots[:, 4:], HALF, 2))
    ref[first : first + slots.shape[0], :, 1024:1152] = both.astype(BF16)


def block_diagonal(w_ref):
    zero = jnp.zeros((HALF, HALF), F32)
    top = jnp.concatenate([w_ref[0], zero], axis=1)
    bottom = jnp.concatenate([zero, w_ref[1]], axis=1)
    return jnp.concatenate([top, bottom], axis=0)


def head_sums(x):
    lane = lax.broadcasted_iota(jnp.int32, x.shape, 1)
    first = jnp.sum(jnp.where(lane < HALF, x, 0.0), axis=1, keepdims=True)
    second = jnp.sum(jnp.where(lane < HALF, 0.0, x), axis=1, keepdims=True)
    return jnp.where(lane < HALF, first, second)


def pick_rows(total, inner):
    out_row = lax.broadcasted_iota(jnp.int32, (total, total), 0)
    in_row = lax.broadcasted_iota(jnp.int32, (total, total), 1)
    outer = total // inner
    wanted = (out_row & (outer - 1)) * inner + (out_row >> int(math.log2(outer)))
    return jnp.where(wanted == in_row, 1.0, 0.0).astype(BF16)


def chunks(width):
    return [(start, min(width, start + 256)) for start in range(0, width, 256)]


def to_blocks(rows_ref, source_ref, pieces, blocks):
    half = pieces // 2
    total = half * blocks
    pick = pick_rows(total, blocks)
    for start, stop in chunks(source_ref.shape[1]):
        for h in range(2):
            moved = dot(pick, source_ref[h * total : (h + 1) * total, start:stop], ((1,), (0,)))
            moved = moved.astype(BF16)
            for j in range(blocks):
                at = j * pieces + h * half
                rows_ref[at : at + half, start:stop] = moved[j * half : (j + 1) * half]


def half_to_pieces(pick, rows_ref, pieces, blocks, h, start, stop):
    half = pieces // 2
    part = [
        rows_ref[j * pieces + h * half : j * pieces + (h + 1) * half, start:stop]
        for j in range(blocks)
    ]
    return dot(pick, jnp.concatenate(part, axis=0), ((1,), (0,)))


def fold(block, pieces):
    return jnp.concatenate(
        [block[c * pieces : (c + 1) * pieces, :] for c in range(block.shape[0] // pieces)], axis=1
    )


def unfold(rows):
    return jnp.concatenate(
        [rows[:, c * LANES : (c + 1) * LANES] for c in range(rows.shape[1] // LANES)], axis=0
    )


def pack_kernel(
    partner_hbm,
    q_hbm,
    k_hbm,
    g_hbm,
    delta_hbm,
    out_ref,
    summary_ref,
    rows_ref,
    partner_ref,
    q_ref,
    k_ref,
    g_ref,
    delta_ref,
    sems,
    small_sems,
):
    blocks, pieces, block_len = 8, 64, 256
    score_scale = 1.0 / math.sqrt(HALF)
    pool_scale = 1.0 / math.sqrt(block_len)
    copies = []
    for half in range(2):
        at = pl.ds(half * blocks // 2 * block_len, blocks // 2 * block_len)
        pairs = ((k_hbm, k_ref), (q_hbm, q_ref), (g_hbm, g_ref))
        copies.append(
            [
                pltpu.make_async_copy(there.at[at], here.at[at], sems.at[half, i])
                for i, (there, here) in enumerate(pairs)
            ]
        )
    copies[0] += [
        pltpu.make_async_copy(delta_hbm, delta_ref, small_sems.at[0]),
        pltpu.make_async_copy(partner_hbm, partner_ref, small_sems.at[1]),
    ]
    for copy in copies[0] + copies[1]:
        copy.start()

    for j in range(blocks):
        if j % (blocks // 2) == 0:
            for copy in copies[j // (blocks // 2)]:
                copy.wait()
        at = slice(j * block_len, (j + 1) * block_len)
        qb, kb, gb = q_ref[at, :], k_ref[at, :], g_ref[at, :]
        scores = dot(kb, head_stack(qb, score_scale), ((1,), (1,)))
        top = jnp.max(scores, axis=0, keepdims=True)
        lse = top + jnp.log(jnp.sum(jnp.exp(scores - top), axis=0, keepdims=True))
        summary = jnp.sum(kb.astype(F32), axis=0, keepdims=True) * pool_scale
        summary_ref[j : j + 1, :] = summary
        delta = jnp.concatenate([delta_ref[0:1, at], delta_ref[1:2, at]], axis=1)
        stats = jnp.concatenate([to_rows(lse), to_rows(delta)], axis=0)
        parts = jnp.concatenate(split3(stats), axis=0)
        summary_parts = jnp.concatenate(
            list(split3(head_rows(summary))) + [jnp.zeros((10, HALF), F32)], axis=0
        )
        left = jnp.concatenate([parts, summary_parts], axis=0)
        lane = lax.broadcasted_iota(jnp.int32, (pieces, HALF), 1)
        place = partner_ref[j]
        right = jnp.where(
            lane == 0,
            (place >> 3).astype(F32),
            jnp.where(lane == 1, (place & 7).astype(F32), 0.0),
        )
        to = slice(j * pieces, (j + 1) * pieces)
        rows_ref[to, 0:512] = fold(qb, pieces)
        rows_ref[to, 512:1024] = fold(gb, pieces)
        rows_ref[to, 1024:1152] = jnp.concatenate([left, right], axis=1).astype(BF16)

    pick = pick_rows(rows_ref.shape[0] // 2, pieces // 2)
    for start, stop in chunks(1152):
        for h in range(2):
            moved = half_to_pieces(pick, rows_ref, pieces, blocks, h, start, stop)
            out_ref[h * 256 : (h + 1) * 256, start:stop] = moved.astype(BF16)


def partner_pick(place):
    rows = place.shape[1]
    row = lax.broadcasted_iota(jnp.int32, (rows, rows), 0).astype(F32)
    return jnp.where(row == place, 1.0, 0.0).astype(BF16)


def forward_kernel(in_ref, out_ref, place_ref):
    tags = in_ref[:, 1024:1152].astype(F32).T
    place = tags[HALF : HALF + 1, :] * 8.0 + tags[HALF + 1 : HALF + 2, :]
    place_ref[...] = place
    pick = partner_pick(place)
    for start in range(0, 1152, 256):
        stop = min(1152, start + 256)
        out_ref[:, start:stop] = dot(pick, in_ref[:, start:stop], ((1,), (0,))).astype(BF16)


def backward_kernel(place_ref, in_ref, out_ref):
    pick = partner_pick(place_ref[...])
    rows = pick.shape[0]
    for start in (0, 256):
        part = load_slots(in_ref, start, start + 256, 512).astype(BF16)
        store_slots(out_ref, 0, dot(pick, part, ((0,), (0,))), start, start + 256, 512)
    tail = load_slot_stats(in_ref)
    moved = dot(pick, tail.astype(BF16), ((0,), (0,)))
    total = jnp.sum(tail.reshape(rows // 8, 8, LANES), axis=0)
    lane8 = lax.broadcasted_iota(jnp.int32, (8, LANES), 1)
    total = total + pltpu.roll(total, LANES - SHARE, 1)
    total = jnp.where((lane8 >= QUARTER) & (lane8 < QUARTER + SHARE), total, 0.0)
    high, mid, _ = split3(total)
    share = high + pltpu.roll(mid, SHARE, 1)
    share = jnp.broadcast_to(share[None], (rows // 8, 8, LANES)).reshape(rows, LANES)
    lane = lax.broadcasted_iota(jnp.int32, (rows, LANES), 1)
    store_slot_stats(out_ref, 0, jnp.where(lane < QUARTER, moved, share))


def far_kernel(
    in_ref,
    k_ref,
    v_ref,
    summary_ref,
    w_ref,
    out_ref,
    dk_ref,
    dv_ref,
    column_ref,
    rows_ref,
    back_ref,
    gate_ref,
    grad_ref,
):
    blocks, pieces, block_len = 8, 64, 256
    score_scale = 1.0 / math.sqrt(HALF)
    to_blocks(rows_ref, in_ref, pieces, blocks)
    arrived = []
    for j in range(blocks):
        s = rows_ref[j * pieces + 48 : j * pieces + 64, 1024:1152].astype(F32)[:, :HALF]
        arrived.append(from_head_rows(s[0:2] + s[2:4] + s[4:6]))
    summary_in = jnp.concatenate(arrived, axis=0)
    summary = summary_ref[...]
    sortq = dot(summary_in, block_diagonal(w_ref), ((1,), (0,)), precision=lax.Precision.HIGHEST)
    gates = jax.nn.sigmoid(score_scale * head_sums(sortq * summary))
    gate_ref[...] = gates

    def step(j, carry):
        at = pl.ds(pl.multiple_of(j * block_len, block_len), block_len)
        here = pl.ds(pl.multiple_of(j * pieces, pieces), pieces)
        kb, vb = k_ref[at, :], v_ref[at, :]
        qs = head_stack(unfold(rows_ref[here, 0:512]), score_scale)
        gs = head_stack(unfold(rows_ref[here, 512:1024]), 1.0)
        stats = rows_ref[here, 1024:1152].astype(F32)
        joined = stats[0:16, :HALF] + stats[16:32, :HALF] + stats[32:48, :HALF]
        own_lse = from_rows(joined[0:8])
        delta = from_rows(joined[8:16])
        gate = gate_ref[pl.ds(j, 1), :]
        gate_row = jnp.concatenate(
            [
                jnp.broadcast_to(gate[:, 0:1], (1, block_len)),
                jnp.broadcast_to(gate[:, HALF : HALF + 1], (1, block_len)),
            ],
            axis=1,
        )
        scores = dot(kb, qs, ((1,), (1,)))
        top = jnp.maximum(own_lse, jnp.max(scores, axis=0, keepdims=True))
        weights = jnp.exp(scores - top)
        total = jnp.exp(own_lse - top) + jnp.sum(weights, axis=0, keepdims=True)
        probs = weights * (1.0 / total)
        lse = top + jnp.log(total)
        low = probs.astype(BF16)
        dprobs = dot(vb, gs, ((1,), (1,)))
        dscores = (probs * (gate_row * dprobs - delta)).astype(BF16)
        dk_ref[at, :] = dot(dscores, qs, ((1,), (0,))).astype(BF16)
        dv = dot(low, gs, ((1,), (0,)))
        dv_ref[at, :] = (dv * gate).astype(BF16)
        grad_ref[pl.ds(j, 1), :] = jnp.sum(dv * vb.astype(F32), axis=0, keepdims=True)
        dq = dot(kb, dscores, ((0,), (0,))) * score_scale
        dq = jnp.concatenate([dq[:HALF, :block_len], dq[HALF:, block_len:]], axis=1)
        back_ref[here, 0:512] = dq.astype(BF16)
        parts = jnp.concatenate(
            list(split3(narrow(to_rows(lse)))) + [jnp.zeros((16, QUARTER), F32)], axis=0
        )
        back_ref[here, 512:640] = jnp.concatenate(
            [parts, jnp.zeros((pieces, LANES - QUARTER), F32)], axis=1
        ).astype(BF16)
        return carry

    lax.fori_loop(0, blocks, step, 0, unroll=True)
    logit_grad = head_sums(grad_ref[...]) * gates * (1.0 - gates)
    sortq_grad = score_scale * logit_grad * summary
    column_ref[...] = score_scale * logit_grad * sortq
    for j in range(blocks):
        parts = jnp.concatenate(
            list(split3(narrow(head_rows(sortq_grad[j : j + 1, :]))))
            + [jnp.zeros((4, QUARTER), F32)],
            axis=0,
        )
        back_ref[j * pieces + 48 : (j + 1) * pieces, 512:640] = jnp.concatenate(
            [parts, jnp.zeros((16, LANES - QUARTER), F32)], axis=1
        ).astype(BF16)
    outer = dot(summary_in, sortq_grad, ((0,), (0,)), precision=lax.Precision.HIGHEST)
    lane = lax.broadcasted_iota(jnp.int32, (LANES, LANES), 1)
    row = lax.broadcasted_iota(jnp.int32, (LANES, LANES), 0)
    outer = jnp.where(row < HALF, outer, pltpu.roll(outer, HALF, 1))
    inside = (lane >= QUARTER) & (lane < QUARTER + SHARE)
    shares = []
    for a in range(4):
        part = jnp.where(inside, pltpu.roll(outer, (QUARTER - SHARE * a) % LANES, 1), 0.0)
        high, mid, _ = split3(part)
        shares.append(high + pltpu.roll(mid, SHARE, 1))
    pick = pick_rows(rows_ref.shape[0] // 2, pieces // 2)
    for h in range(2):
        for start in (0, 256):
            moved = half_to_pieces(pick, back_ref, pieces, blocks, h, start, start + 256)
            store_slots(out_ref, h * pieces // 2, moved, start, start + 256, 512)
        moved = half_to_pieces(pick, back_ref, pieces, blocks, h, 512, 640)
        moved = moved + jnp.concatenate(shares[2 * h : 2 * h + 2], axis=0)
        store_slot_stats(out_ref, h * pieces // 2, moved)


def self_kernel(
    in_ref,
    q_ref,
    k_ref,
    v_ref,
    g_ref,
    delta_ref,
    w_ref,
    dk_far_ref,
    dv_far_ref,
    column_ref,
    dq_hbm,
    dk_hbm,
    dv_hbm,
    sort_out,
    rows_ref,
    dq_out,
    dk_out,
    dv_out,
    sems,
    natural_ref,
):
    blocks, pieces, block_len = 8, 64, 256
    score_scale = 1.0 / math.sqrt(HALF)
    pool_scale = 1.0 / math.sqrt(block_len)
    for start in (0, 256):
        part = load_slots(in_ref, start, start + 256, 512)
        natural_ref[:, start : start + 256] = part.astype(BF16)
    natural_ref[:, 512:640] = load_slot_stats(in_ref).astype(BF16)
    to_blocks(rows_ref, natural_ref, pieces, blocks)
    arrived = []
    for j in range(blocks):
        s = rows_ref[j * pieces + 48 : (j + 1) * pieces, 512:640].astype(F32)[:, :QUARTER]
        arrived.append(from_head_rows(widen(s[0:4] + s[4:8] + s[8:12])))
    sortq_grad = jnp.concatenate(arrived, axis=0)
    row_grad = dot(
        sortq_grad, block_diagonal(w_ref), ((1,), (1,)), precision=lax.Precision.HIGHEST
    )
    extra = pool_scale * (row_grad + column_ref[...])

    lane = lax.broadcasted_iota(jnp.int32, (LANES, LANES), 1)
    found = jnp.zeros((LANES, LANES), F32)
    for a in range(4):
        s = natural_ref[a * LANES : (a + 1) * LANES, 512:640].astype(F32)
        s = s + pltpu.roll(s, LANES - SHARE, 1)
        s = pltpu.roll(s, (SHARE * a - QUARTER) % LANES, 1)
        inside = (lane >= SHARE * a) & (lane < SHARE * (a + 1))
        found = found + jnp.where(inside, s, 0.0)
    sort_out[...] = found[:, :HALF]

    copies = []
    for j in range(blocks):
        at = slice(j * block_len, (j + 1) * block_len)
        here = slice(j * pieces, (j + 1) * pieces)
        kb, vb = k_ref[at, :], v_ref[at, :]
        qs = head_stack(q_ref[at, :], score_scale)
        gs = head_stack(g_ref[at, :], 1.0)
        far = rows_ref[here, 0:512].astype(F32)
        stats = rows_ref[here, 512:640].astype(F32)
        stats = stats[:, :QUARTER]
        lse = from_rows(widen(stats[0:16] + stats[16:32] + stats[32:48]))
        delta = jnp.concatenate([delta_ref[0:1, at], delta_ref[1:2, at]], axis=1)
        scores = dot(kb, qs, ((1,), (1,)))
        probs = jnp.exp(scores - lse)
        low = probs.astype(BF16)
        dprobs = dot(vb, gs, ((1,), (1,)))
        dscores = (probs * (dprobs - delta)).astype(BF16)
        dk = dot(dscores, qs, ((1,), (0,)))
        dk_out[at, :] = (dk + dk_far_ref[at, :].astype(F32) + extra[j : j + 1, :]).astype(BF16)
        dv = dot(low, gs, ((1,), (0,)))
        dv_out[at, :] = (dv + dv_far_ref[at, :].astype(F32)).astype(BF16)
        dq = dot(kb, dscores, ((0,), (0,))) * score_scale
        dq = jnp.concatenate(
            [
                dq[:HALF, :block_len] + far[:, :block_len],
                dq[HALF:, block_len:] + far[:, block_len:],
            ],
            axis=0,
        )
        dq_out[at, :] = dq.T.astype(BF16)
        if j % (blocks // 2) == blocks // 2 - 1:
            half = j // (blocks // 2)
            rows = pl.ds(half * blocks // 2 * block_len, blocks // 2 * block_len)
            pairs = ((dq_out, dq_hbm), (dk_out, dk_hbm), (dv_out, dv_hbm))
            for i, (here_ref, there) in enumerate(pairs):
                copy = pltpu.make_async_copy(here_ref.at[rows], there.at[rows], sems.at[half, i])
                copy.start()
                copies.append(copy)

    for copy in copies:
        copy.wait()


def whole(memory_space=pltpu.VMEM):
    return pl.BlockSpec(memory_space=memory_space)


def call(
    kernel, outs, inputs, scratch=(), in_hbm=False, out_hbm=0, limit=VMEM_LIMIT, flops=1 << 28
):
    shapes = [jax.ShapeDtypeStruct(shape, dtype) for shape, dtype in outs]
    size = sum(math.prod(s.shape) * s.dtype.itemsize for s in shapes)
    size += sum(x.size * x.dtype.itemsize for x in inputs)
    return pl.pallas_call(
        kernel,
        out_shape=shapes,
        in_specs=[whole(pl.ANY if in_hbm else pltpu.VMEM)] * len(inputs),
        out_specs=[whole(pl.ANY)] * out_hbm + [whole()] * (len(shapes) - out_hbm),
        scratch_shapes=list(scratch),
        compiler_params=pltpu.CompilerParams(vmem_limit_bytes=limit),
        cost_estimate=pl.CostEstimate(flops=flops, bytes_accessed=size, transcendentals=1 << 20),
    )(*inputs)


def exchange(x):
    return lax.all_to_all(x, "seq", split_axis=0, concat_axis=0, tiled=True)


def per_device(queries, keys, values, delta, dout, partner, sort_weight):
    tokens = queries.shape[0]
    rows = lax.axis_size("seq") * partner.shape[0]
    blocks = partner.shape[0]
    buffer = pltpu.VMEM((tokens, LANES), BF16)
    sent, summary = call(
        pack_kernel,
        [((rows, 1152), BF16), ((blocks, LANES), F32)],
        [partner, queries, keys, dout, delta],
        scratch=[
            pltpu.VMEM((rows, 1152), BF16),
            pltpu.SMEM((blocks,), jnp.int32),
            buffer,
            buffer,
            buffer,
            pltpu.VMEM(delta.shape, F32),
            pltpu.SemaphoreType.DMA((2, 3)),
            pltpu.SemaphoreType.DMA((2,)),
        ],
        in_hbm=True,
        limit=WHOLE_LIMIT,
    )
    spread = exchange(sent)
    moved, place = call(
        forward_kernel, [((rows, 1152), BF16), ((1, rows), F32)], [spread]
    )
    arrived = exchange(moved)
    slots = ((rows // blocks, 4, 1152), BF16)
    back, dk_far, dv_far, column = call(
        far_kernel,
        [
            slots,
            ((tokens, LANES), BF16),
            ((tokens, LANES), BF16),
            ((8, LANES), F32),
        ],
        [arrived, keys, values, summary, sort_weight],
        scratch=[
            pltpu.VMEM((rows, 1152), BF16),
            pltpu.VMEM((rows, 640), BF16),
            pltpu.VMEM((8, LANES), F32),
            pltpu.VMEM((8, LANES), F32),
        ],
    )
    spread_back = exchange(back)
    (moved_back,) = call(backward_kernel, [slots], [place, spread_back])
    arrived_back = exchange(moved_back)
    d_queries, d_keys, d_values, d_sort = call(
        self_kernel,
        [((tokens, LANES), BF16)] * 3 + [((LANES, HALF), F32)],
        [
            arrived_back,
            queries,
            keys,
            values,
            dout,
            delta,
            sort_weight,
            dk_far,
            dv_far,
            column,
        ],
        scratch=[
            pltpu.VMEM((rows, 640), BF16),
            buffer,
            buffer,
            buffer,
            pltpu.SemaphoreType.DMA((2, 3)),
            pltpu.VMEM((rows, 640), BF16),
        ],
        out_hbm=3,
    )
    return d_queries, d_keys, d_values, d_sort.reshape(sort_weight.shape)


def solution(mesh):
    in_specs = (
        P("seq", "head"),
        P("seq", "head"),
        P("seq", "head"),
        P("head", "seq"),
        P("seq", "head"),
        P("seq"),
        P("head", None, None),
    )
    out_specs = (P("seq", "head"), P("seq", "head"), P("seq", "head"), P("head", None, None))
    return jax.shard_map(
        per_device, mesh=mesh, in_specs=in_specs, out_specs=out_specs, check_vma=False
    )
```

```python
import functools
import math

import jax
import jax.numpy as jnp
from jax import lax
from jax.experimental import pallas as pl
from jax.experimental.pallas import tpu as pltpu
from jax.sharding import PartitionSpec as P

F32 = jnp.float32
BF16 = jnp.bfloat16
LANES = 128
HALF = 64
QUARTER = 32
SHARE = 16
TAGS = 48
VMEM_LIMIT = 48 * 1024 * 1024
WHOLE_LIMIT = 62240000


def dot(a, b, dims, **kw):
    return lax.dot_general(a, b, (dims, ((), ())), preferred_element_type=F32, **kw)


def head_stack(x, scale):
    lane = lax.broadcasted_iota(jnp.int32, (1, LANES), 1)
    first = jnp.where(lane < HALF, scale, 0.0).astype(BF16)
    second = jnp.where(lane < HALF, 0.0, scale).astype(BF16)
    return jnp.concatenate([x * first, x * second], axis=0)


def split3(x):
    high = x.astype(BF16).astype(F32)
    rest = x - high
    mid = rest.astype(BF16).astype(F32)
    return high, mid, (rest - mid).astype(BF16).astype(F32)


def to_rows(v):
    return jnp.concatenate([v[:, i * HALF : (i + 1) * HALF] for i in range(8)], axis=0)


def from_rows(x):
    return jnp.concatenate([x[i : i + 1, :] for i in range(8)], axis=1)


def head_rows(v):
    return jnp.concatenate([v[:, :HALF], v[:, HALF:]], axis=0)


def from_head_rows(x):
    return jnp.concatenate([x[0:1, :], x[1:2, :]], axis=1)


def narrow(x):
    width = x.shape[1] // 2
    return jnp.concatenate([x[:, :width], x[:, width:]], axis=0)


def widen(x):
    rows = x.shape[0] // 2
    return jnp.concatenate([x[:rows], x[rows:]], axis=1)


def load_half(ref, half, start, stop, step):
    part = ref[:, :, start + half * step : stop + half * step].astype(F32)
    return part.reshape(part.shape[0] * 4, stop - start).astype(BF16)


def load_half_stats(ref, half, at):
    part = ref[:, :, at : at + LANES].astype(F32).reshape(ref.shape[0] * 4, LANES)
    return pltpu.roll(part, HALF, 1) if half else part


def store_half(ref, half, rows, start, stop, step):
    slots = rows.reshape(ref.shape[0], 4, stop - start).astype(BF16)
    ref[:, :, start + half * step : stop + half * step] = slots


def store_stats(ref, at, low, high):
    lane = lax.broadcasted_iota(jnp.int32, low.shape, 1)
    both = jnp.where(lane < HALF, low, pltpu.roll(high, HALF, 1))
    ref[:, :, at : at + LANES] = both.reshape(ref.shape[0], 4, LANES).astype(BF16)


def block_diagonal(w_ref):
    zero = jnp.zeros((HALF, HALF), F32)
    top = jnp.concatenate([w_ref[0], zero], axis=1)
    bottom = jnp.concatenate([zero, w_ref[1]], axis=1)
    return jnp.concatenate([top, bottom], axis=0)


def head_sums(x):
    lane = lax.broadcasted_iota(jnp.int32, x.shape, 1)
    first = jnp.sum(jnp.where(lane < HALF, x, 0.0), axis=1, keepdims=True)
    second = jnp.sum(jnp.where(lane < HALF, 0.0, x), axis=1, keepdims=True)
    return jnp.where(lane < HALF, first, second)


def pick_rows(total, inner):
    out_row = lax.broadcasted_iota(jnp.int32, (total, total), 0)
    in_row = lax.broadcasted_iota(jnp.int32, (total, total), 1)
    outer = total // inner
    wanted = (out_row & (outer - 1)) * inner + (out_row >> int(math.log2(outer)))
    return jnp.where(wanted == in_row, 1.0, 0.0).astype(BF16)


def chunks(width):
    return [(start, start + 256) for start in range(0, width, 256)]


def send_rows(out_ref, rows_ref, width, extra):
    half_rows = rows_ref.shape[0] // 2
    pick = pick_rows(half_rows, half_rows // 4)
    tails = []
    for h in range(2):
        at = slice(h * half_rows, (h + 1) * half_rows)
        for start, stop in chunks(width):
            moved = dot(pick, rows_ref[at, start:stop], ((1,), (0,)))
            store_half(out_ref, h, moved, start, stop, width)
        tails.append(dot(pick, rows_ref[at, width : width + LANES], ((1,), (0,))))
        if extra is not None:
            tails[h] = tails[h] + extra[h]
    store_stats(out_ref, 2 * width, *tails)


def receive_rows(rows_ref, in_ref, width):
    half_rows = rows_ref.shape[0] // 2
    pick = pick_rows(half_rows, 4)
    tails = []
    for h in range(2):
        at = slice(h * half_rows, (h + 1) * half_rows)
        for start, stop in chunks(width):
            part = load_half(in_ref, h, start, stop, width)
            rows_ref[at, start:stop] = dot(pick, part, ((1,), (0,))).astype(BF16)
        tails.append(load_half_stats(in_ref, h, 2 * width))
        moved = dot(pick, tails[h].astype(BF16), ((1,), (0,)))
        rows_ref[at, width : width + LANES] = moved.astype(BF16)
    return tails


def fold(block, pieces):
    return jnp.concatenate(
        [block[c * pieces : (c + 1) * pieces, :] for c in range(block.shape[0] // pieces)], axis=1
    )


def unfold(rows):
    return jnp.concatenate(
        [rows[:, c * LANES : (c + 1) * LANES] for c in range(rows.shape[1] // LANES)], axis=0
    )


def pack_kernel(
    partner_hbm,
    q_hbm,
    k_hbm,
    g_hbm,
    delta_hbm,
    out_ref,
    summary_ref,
    rows_ref,
    partner_ref,
    q_ref,
    k_ref,
    g_ref,
    delta_ref,
    sems,
    small_sems,
):
    blocks, pieces, block_len = 8, 64, 256
    score_scale = 1.0 / math.sqrt(HALF)
    pool_scale = 1.0 / math.sqrt(block_len)
    copies = []
    for half in range(2):
        at = pl.ds(half * blocks // 2 * block_len, blocks // 2 * block_len)
        pairs = ((k_hbm, k_ref), (q_hbm, q_ref), (g_hbm, g_ref))
        copies.append(
            [
                pltpu.make_async_copy(there.at[at], here.at[at], sems.at[half, i])
                for i, (there, here) in enumerate(pairs)
            ]
        )
    copies[0] += [
        pltpu.make_async_copy(delta_hbm, delta_ref, small_sems.at[0]),
        pltpu.make_async_copy(partner_hbm, partner_ref, small_sems.at[1]),
    ]
    for copy in copies[0] + copies[1]:
        copy.start()

    for j in range(blocks):
        if j % (blocks // 2) == 0:
            for copy in copies[j // (blocks // 2)]:
                copy.wait()
        at = slice(j * block_len, (j + 1) * block_len)
        qb, kb, gb = q_ref[at, :], k_ref[at, :], g_ref[at, :]
        scores = dot(kb, head_stack(qb, score_scale), ((1,), (1,)))
        top = jnp.max(scores, axis=0, keepdims=True)
        lse = top + jnp.log(jnp.sum(jnp.exp(scores - top), axis=0, keepdims=True))
        summary = jnp.sum(kb.astype(F32), axis=0, keepdims=True) * pool_scale
        summary_ref[j : j + 1, :] = summary
        delta = jnp.concatenate([delta_ref[0:1, at], delta_ref[1:2, at]], axis=1)
        left = jnp.concatenate(
            list(split3(narrow(to_rows(lse))))
            + list(split3(narrow(head_rows(summary))))
            + [jnp.zeros((4, QUARTER), F32)],
            axis=0,
        )
        deltas = jnp.concatenate(split3(narrow(narrow(to_rows(delta))))[:2], axis=0)
        lane = lax.broadcasted_iota(jnp.int32, (pieces, LANES - TAGS), 1)
        place = partner_ref[j]
        high = ((place & 4) << 4) | (place >> 3)
        tags = jnp.where(
            lane == 0,
            high.astype(F32),
            jnp.where(lane == 1, (place & 3).astype(F32), 0.0),
        )
        to = slice(j * pieces, (j + 1) * pieces)
        rows_ref[to, 0:512] = fold(qb, pieces)
        rows_ref[to, 512:1024] = fold(gb, pieces)
        rows_ref[to, 1024:1152] = jnp.concatenate([left, deltas, tags], axis=1).astype(BF16)

    send_rows(out_ref, rows_ref, 1024, None)


def partner_pick(place):
    rows = place.shape[1]
    row = lax.broadcasted_iota(jnp.int32, (rows, rows), 0).astype(F32)
    return jnp.where(row == place, 1.0, 0.0).astype(BF16)


def forward_kernel(in_ref, out_ref, place_ref):
    tail = jnp.concatenate([load_half_stats(in_ref, h, 2048) for h in range(2)], axis=0)
    tags = tail.T
    place = tags[TAGS : TAGS + 1, :] * 4.0 + tags[TAGS + 1 : TAGS + 2, :]
    place_ref[...] = place
    pick = partner_pick(place)
    half_rows = tail.shape[0] // 2
    for start, stop in chunks(1024):
        part = jnp.concatenate(
            [load_half(in_ref, h, start, stop, 1024) for h in range(2)], axis=0
        )
        moved = dot(pick, part, ((1,), (0,)))
        store_half(out_ref, 0, moved[:half_rows], start, stop, 1024)
        store_half(out_ref, 1, moved[half_rows:], start, stop, 1024)
    moved = dot(pick, tail.astype(BF16), ((1,), (0,)))
    store_stats(out_ref, 2048, moved[:half_rows], moved[half_rows:])


def backward_kernel(place_ref, in_ref, out_ref):
    pick = partner_pick(place_ref[...])
    half_rows = pick.shape[0] // 2
    for start, stop in chunks(512):
        part = jnp.concatenate(
            [load_half(in_ref, h, start, stop, 512) for h in range(2)], axis=0
        )
        moved = dot(pick, part, ((0,), (0,)))
        store_half(out_ref, 0, moved[:half_rows], start, stop, 512)
        store_half(out_ref, 1, moved[half_rows:], start, stop, 512)
    tails = [load_half_stats(in_ref, h, 1024) for h in range(2)]
    moved = dot(pick, jnp.concatenate(tails, axis=0).astype(BF16), ((0,), (0,)))
    lane8 = lax.broadcasted_iota(jnp.int32, (8, LANES), 1)
    lane = lax.broadcasted_iota(jnp.int32, (half_rows, LANES), 1)
    sent = []
    for h in range(2):
        total = jnp.sum(tails[h].reshape(half_rows // 8, 8, LANES), axis=0)
        total = total + pltpu.roll(total, 4, 0)
        total = total + pltpu.roll(total, LANES - SHARE, 1)
        total = jnp.where((lane8 >= QUARTER) & (lane8 < QUARTER + SHARE), total, 0.0)
        high, mid, _ = split3(total)
        share = high + pltpu.roll(mid, SHARE, 1)
        share = jnp.broadcast_to(share[None], (half_rows // 8, 8, LANES))
        share = share.reshape(half_rows, LANES)
        at = slice(h * half_rows, (h + 1) * half_rows)
        sent.append(jnp.where(lane < QUARTER, moved[at], share))
    store_stats(out_ref, 1024, *sent)


def far_kernel(
    in_ref,
    k_ref,
    v_ref,
    summary_ref,
    w_ref,
    out_ref,
    dk_ref,
    dv_ref,
    column_ref,
    rows_ref,
    back_ref,
    gate_ref,
    grad_ref,
):
    blocks, pieces, block_len = 8, 64, 256
    score_scale = 1.0 / math.sqrt(HALF)
    receive_rows(rows_ref, in_ref, 1024)
    arrived = []
    for j in range(blocks):
        s = rows_ref[j * pieces + 48 : (j + 1) * pieces, 1024:1152].astype(F32)[:, :QUARTER]
        arrived.append(from_head_rows(widen(s[0:4] + s[4:8] + s[8:12])))
    summary_in = jnp.concatenate(arrived, axis=0)
    summary = summary_ref[...]
    sortq = dot(summary_in, block_diagonal(w_ref), ((1,), (0,)), precision=lax.Precision.HIGHEST)
    gates = jax.nn.sigmoid(score_scale * head_sums(sortq * summary))
    gate_ref[...] = gates

    def step(j, carry):
        at = pl.ds(pl.multiple_of(j * block_len, block_len), block_len)
        here = pl.ds(pl.multiple_of(j * pieces, pieces), pieces)
        kb, vb = k_ref[at, :], v_ref[at, :]
        qs = head_stack(unfold(rows_ref[here, 0:512]), score_scale)
        gs = head_stack(unfold(rows_ref[here, 512:1024]), 1.0)
        stats = rows_ref[here, 1024:1152].astype(F32)
        parts = stats[:, :QUARTER]
        own_lse = from_rows(widen(parts[0:16] + parts[16:32] + parts[32:48]))
        parts = stats[:, QUARTER:TAGS]
        delta = from_rows(widen(widen(parts[0:32] + parts[32:64])))
        gate = gate_ref[pl.ds(j, 1), :]
        gate_row = jnp.concatenate(
            [
                jnp.broadcast_to(gate[:, 0:1], (1, block_len)),
                jnp.broadcast_to(gate[:, HALF : HALF + 1], (1, block_len)),
            ],
            axis=1,
        )
        scores = dot(kb, qs, ((1,), (1,)))
        top = jnp.maximum(own_lse, jnp.max(scores, axis=0, keepdims=True))
        weights = jnp.exp(scores - top)
        total = jnp.exp(own_lse - top) + jnp.sum(weights, axis=0, keepdims=True)
        probs = weights * (1.0 / total)
        lse = top + jnp.log(total)
        low = probs.astype(BF16)
        dprobs = dot(vb, gs, ((1,), (1,)))
        dscores = (probs * (gate_row * dprobs - delta)).astype(BF16)
        dk_ref[at, :] = dot(dscores, qs, ((1,), (0,))).astype(BF16)
        dv = dot(low, gs, ((1,), (0,)))
        dv_ref[at, :] = (dv * gate).astype(BF16)
        grad_ref[pl.ds(j, 1), :] = jnp.sum(dv * vb.astype(F32), axis=0, keepdims=True)
        dq = dot(kb, dscores, ((0,), (0,))) * score_scale
        dq = jnp.concatenate([dq[:HALF, :block_len], dq[HALF:, block_len:]], axis=1)
        back_ref[here, 0:512] = dq.astype(BF16)
        parts = jnp.concatenate(
            list(split3(narrow(to_rows(lse)))) + [jnp.zeros((16, QUARTER), F32)], axis=0
        )
        back_ref[here, 512:640] = jnp.concatenate(
            [parts, jnp.zeros((pieces, LANES - QUARTER), F32)], axis=1
        ).astype(BF16)
        return carry

    lax.fori_loop(0, blocks, step, 0, unroll=True)
    logit_grad = head_sums(grad_ref[...]) * gates * (1.0 - gates)
    sortq_grad = score_scale * logit_grad * summary
    column_ref[...] = score_scale * logit_grad * sortq
    for j in range(blocks):
        parts = jnp.concatenate(
            list(split3(narrow(head_rows(sortq_grad[j : j + 1, :]))))
            + [jnp.zeros((4, QUARTER), F32)],
            axis=0,
        )
        back_ref[j * pieces + 48 : (j + 1) * pieces, 512:640] = jnp.concatenate(
            [parts, jnp.zeros((16, LANES - QUARTER), F32)], axis=1
        ).astype(BF16)
    outer = dot(summary_in, sortq_grad, ((0,), (0,)), precision=lax.Precision.HIGHEST)
    lane = lax.broadcasted_iota(jnp.int32, (LANES, LANES), 1)
    row = lax.broadcasted_iota(jnp.int32, (LANES, LANES), 0)
    outer = jnp.where(row < HALF, outer, pltpu.roll(outer, HALF, 1))
    inside = (lane >= QUARTER) & (lane < QUARTER + SHARE)
    shares = []
    for a in range(4):
        part = jnp.where(inside, pltpu.roll(outer, (QUARTER - SHARE * a) % LANES, 1), 0.0)
        high, mid, _ = split3(part)
        shares.append(high + pltpu.roll(mid, SHARE, 1))
    extra = [jnp.concatenate(shares[2 * h : 2 * h + 2], axis=0) for h in range(2)]
    send_rows(out_ref, back_ref, 512, extra)


def self_kernel(
    in_ref,
    q_ref,
    k_ref,
    v_ref,
    g_ref,
    delta_ref,
    w_ref,
    dk_far_ref,
    dv_far_ref,
    column_ref,
    dq_hbm,
    dk_hbm,
    dv_hbm,
    sort_out,
    rows_ref,
    dq_out,
    dk_out,
    dv_out,
    sems,
):
    blocks, pieces, block_len = 8, 64, 256
    score_scale = 1.0 / math.sqrt(HALF)
    pool_scale = 1.0 / math.sqrt(block_len)
    tails = receive_rows(rows_ref, in_ref, 512)
    arrived = []
    for j in range(blocks):
        s = rows_ref[j * pieces + 48 : (j + 1) * pieces, 512:640].astype(F32)[:, :QUARTER]
        arrived.append(from_head_rows(widen(s[0:4] + s[4:8] + s[8:12])))
    sortq_grad = jnp.concatenate(arrived, axis=0)
    row_grad = dot(
        sortq_grad, block_diagonal(w_ref), ((1,), (1,)), precision=lax.Precision.HIGHEST
    )
    extra = pool_scale * (row_grad + column_ref[...])

    lane = lax.broadcasted_iota(jnp.int32, (LANES, LANES), 1)
    found = jnp.zeros((LANES, LANES), F32)
    for a in range(4):
        s = tails[a // 2][(a % 2) * LANES : (a % 2 + 1) * LANES]
        s = s + pltpu.roll(s, LANES - SHARE, 1)
        s = pltpu.roll(s, (SHARE * a - QUARTER) % LANES, 1)
        inside = (lane >= SHARE * a) & (lane < SHARE * (a + 1))
        found = found + jnp.where(inside, s, 0.0)
    sort_out[...] = found[:, :HALF]

    copies = []
    for j in range(blocks):
        at = slice(j * block_len, (j + 1) * block_len)
        here = slice(j * pieces, (j + 1) * pieces)
        kb, vb = k_ref[at, :], v_ref[at, :]
        qs = head_stack(q_ref[at, :], score_scale)
        gs = head_stack(g_ref[at, :], 1.0)
        far = rows_ref[here, 0:512].astype(F32)
        stats = rows_ref[here, 512:640].astype(F32)
        stats = stats[:, :QUARTER]
        lse = from_rows(widen(stats[0:16] + stats[16:32] + stats[32:48]))
        delta = jnp.concatenate([delta_ref[0:1, at], delta_ref[1:2, at]], axis=1)
        scores = dot(kb, qs, ((1,), (1,)))
        probs = jnp.exp(scores - lse)
        low = probs.astype(BF16)
        dprobs = dot(vb, gs, ((1,), (1,)))
        dscores = (probs * (dprobs - delta)).astype(BF16)
        dk = dot(dscores, qs, ((1,), (0,)))
        dk_out[at, :] = (dk + dk_far_ref[at, :].astype(F32) + extra[j : j + 1, :]).astype(BF16)
        dv = dot(low, gs, ((1,), (0,)))
        dv_out[at, :] = (dv + dv_far_ref[at, :].astype(F32)).astype(BF16)
        dq = dot(kb, dscores, ((0,), (0,))) * score_scale
        dq = jnp.concatenate(
            [
                dq[:HALF, :block_len] + far[:, :block_len],
                dq[HALF:, block_len:] + far[:, block_len:],
            ],
            axis=0,
        )
        dq_out[at, :] = dq.T.astype(BF16)
        if j % (blocks // 2) == blocks // 2 - 1:
            half = j // (blocks // 2)
            rows = pl.ds(half * blocks // 2 * block_len, blocks // 2 * block_len)
            pairs = ((dq_out, dq_hbm), (dk_out, dk_hbm), (dv_out, dv_hbm))
            for i, (here_ref, there) in enumerate(pairs):
                copy = pltpu.make_async_copy(here_ref.at[rows], there.at[rows], sems.at[half, i])
                copy.start()
                copies.append(copy)

    for copy in copies:
        copy.wait()


def whole(memory_space=pltpu.VMEM):
    return pl.BlockSpec(memory_space=memory_space)


def call(
    kernel, outs, inputs, scratch=(), in_hbm=False, out_hbm=0, limit=VMEM_LIMIT, flops=1 << 28
):
    shapes = [jax.ShapeDtypeStruct(shape, dtype) for shape, dtype in outs]
    size = sum(math.prod(s.shape) * s.dtype.itemsize for s in shapes)
    size += sum(x.size * x.dtype.itemsize for x in inputs)
    return pl.pallas_call(
        kernel,
        out_shape=shapes,
        in_specs=[whole(pl.ANY if in_hbm else pltpu.VMEM)] * len(inputs),
        out_specs=[whole(pl.ANY)] * out_hbm + [whole()] * (len(shapes) - out_hbm),
        scratch_shapes=list(scratch),
        compiler_params=pltpu.CompilerParams(vmem_limit_bytes=limit),
        cost_estimate=pl.CostEstimate(flops=flops, bytes_accessed=size, transcendentals=1 << 20),
    )(*inputs)


def exchange(x):
    return lax.all_to_all(x, "seq", split_axis=0, concat_axis=0, tiled=True)


def per_device(queries, keys, values, delta, dout, partner, sort_weight):
    tokens = queries.shape[0]
    rows = lax.axis_size("seq") * partner.shape[0]
    blocks = partner.shape[0]
    buffer = pltpu.VMEM((tokens, LANES), BF16)
    wide_slots = ((rows // blocks, 4, 2176), BF16)
    sent, summary = call(
        pack_kernel,
        [wide_slots, ((blocks, LANES), F32)],
        [partner, queries, keys, dout, delta],
        scratch=[
            pltpu.VMEM((rows, 1152), BF16),
            pltpu.SMEM((blocks,), jnp.int32),
            buffer,
            buffer,
            buffer,
            pltpu.VMEM(delta.shape, F32),
            pltpu.SemaphoreType.DMA((2, 3)),
            pltpu.SemaphoreType.DMA((2,)),
        ],
        in_hbm=True,
        limit=WHOLE_LIMIT,
    )
    spread = exchange(sent)
    moved, place = call(
        forward_kernel, [wide_slots, ((1, rows), F32)], [spread]
    )
    arrived = exchange(moved)
    slots = ((rows // blocks, 4, 1152), BF16)
    back, dk_far, dv_far, column = call(
        far_kernel,
        [
            slots,
            ((tokens, LANES), BF16),
            ((tokens, LANES), BF16),
            ((8, LANES), F32),
        ],
        [arrived, keys, values, summary, sort_weight],
        scratch=[
            pltpu.VMEM((rows, 1152), BF16),
            pltpu.VMEM((rows, 640), BF16),
            pltpu.VMEM((8, LANES), F32),
            pltpu.VMEM((8, LANES), F32),
        ],
    )
    spread_back = exchange(back)
    (moved_back,) = call(backward_kernel, [slots], [place, spread_back])
    arrived_back = exchange(moved_back)
    d_queries, d_keys, d_values, d_sort = call(
        self_kernel,
        [((tokens, LANES), BF16)] * 3 + [((LANES, HALF), F32)],
        [
            arrived_back,
            queries,
            keys,
            values,
            dout,
            delta,
            sort_weight,
            dk_far,
            dv_far,
            column,
        ],
        scratch=[
            pltpu.VMEM((rows, 640), BF16),
            buffer,
            buffer,
            buffer,
            pltpu.SemaphoreType.DMA((2, 3)),
        ],
        out_hbm=3,
    )
    return d_queries, d_keys, d_values, d_sort.reshape(sort_weight.shape)


def solution(mesh):
    in_specs = (
        P("seq", "head"),
        P("seq", "head"),
        P("seq", "head"),
        P("head", "seq"),
        P("seq", "head"),
        P("seq"),
        P("head", None, None),
    )
    out_specs = (P("seq", "head"), P("seq", "head"), P("seq", "head"), P("head", None, None))
    return jax.shard_map(
        per_device, mesh=mesh, in_specs=in_specs, out_specs=out_specs, check_vma=False
    )
```

```python
import functools
import math

import jax
import jax.numpy as jnp
from jax import lax
from jax.experimental import pallas as pl
from jax.experimental.pallas import tpu as pltpu
from jax.sharding import PartitionSpec as P

F32 = jnp.float32
BF16 = jnp.bfloat16
LANES = 128
HALF = 64
QUARTER = 32
SHARE = 16
TAGS = 48
VMEM_LIMIT = 48 * 1024 * 1024
WHOLE_LIMIT = 62240000


def dot(a, b, dims, **kw):
    return lax.dot_general(a, b, (dims, ((), ())), preferred_element_type=F32, **kw)


def head_stack(x, scale):
    lane = lax.broadcasted_iota(jnp.int32, (1, LANES), 1)
    first = jnp.where(lane < HALF, scale, 0.0).astype(BF16)
    second = jnp.where(lane < HALF, 0.0, scale).astype(BF16)
    return jnp.concatenate([x * first, x * second], axis=0)


def split3(x):
    high = x.astype(BF16).astype(F32)
    rest = x - high
    mid = rest.astype(BF16).astype(F32)
    return high, mid, (rest - mid).astype(BF16).astype(F32)


def to_rows(v):
    return jnp.concatenate([v[:, i * HALF : (i + 1) * HALF] for i in range(8)], axis=0)


def from_rows(x):
    return jnp.concatenate([x[i : i + 1, :] for i in range(8)], axis=1)


def head_rows(v):
    return jnp.concatenate([v[:, :HALF], v[:, HALF:]], axis=0)


def from_head_rows(x):
    return jnp.concatenate([x[0:1, :], x[1:2, :]], axis=1)


def narrow(x):
    width = x.shape[1] // 2
    return jnp.concatenate([x[:, :width], x[:, width:]], axis=0)


def widen(x):
    rows = x.shape[0] // 2
    return jnp.concatenate([x[:rows], x[rows:]], axis=1)


def load_half(ref, half, start, stop, step):
    part = ref[:, :, start + half * step : stop + half * step].astype(F32)
    return part.reshape(part.shape[0] * 4, stop - start).astype(BF16)


def load_half_stats(ref, half, at):
    part = ref[:, :, at : at + LANES].astype(F32).reshape(ref.shape[0] * 4, LANES)
    return pltpu.roll(part, HALF, 1) if half else part


def store_half(ref, half, rows, start, stop, step):
    slots = rows.reshape(ref.shape[0], 4, stop - start).astype(BF16)
    ref[:, :, start + half * step : stop + half * step] = slots


def store_stats(ref, at, low, high):
    lane = lax.broadcasted_iota(jnp.int32, low.shape, 1)
    both = jnp.where(lane < HALF, low, pltpu.roll(high, HALF, 1))
    ref[:, :, at : at + LANES] = both.reshape(ref.shape[0], 4, LANES).astype(BF16)


def block_diagonal(w_ref):
    zero = jnp.zeros((HALF, HALF), F32)
    top = jnp.concatenate([w_ref[0], zero], axis=1)
    bottom = jnp.concatenate([zero, w_ref[1]], axis=1)
    return jnp.concatenate([top, bottom], axis=0)


def head_sums(x):
    lane = lax.broadcasted_iota(jnp.int32, x.shape, 1)
    first = jnp.sum(jnp.where(lane < HALF, x, 0.0), axis=1, keepdims=True)
    second = jnp.sum(jnp.where(lane < HALF, 0.0, x), axis=1, keepdims=True)
    return jnp.where(lane < HALF, first, second)


def pick_rows(total, inner):
    out_row = lax.broadcasted_iota(jnp.int32, (total, total), 0)
    in_row = lax.broadcasted_iota(jnp.int32, (total, total), 1)
    outer = total // inner
    wanted = (out_row & (outer - 1)) * inner + (out_row >> int(math.log2(outer)))
    return jnp.where(wanted == in_row, 1.0, 0.0).astype(BF16)


def chunks(width):
    return [(start, start + 256) for start in range(0, width, 256)]


def send_half(out_ref, rows_ref, width, h):
    half_rows = rows_ref.shape[0] // 2
    pick = pick_rows(half_rows, half_rows // 4)
    at = slice(h * half_rows, (h + 1) * half_rows)
    for start, stop in chunks(width):
        moved = dot(pick, rows_ref[at, start:stop], ((1,), (0,)))
        store_half(out_ref, h, moved, start, stop, width)
    return dot(pick, rows_ref[at, width : width + LANES], ((1,), (0,)))


def send_rows(out_ref, rows_ref, width, extra):
    tails = [send_half(out_ref, rows_ref, width, h) + extra[h] for h in range(2)]
    store_stats(out_ref, 2 * width, *tails)


def receive_rows(rows_ref, in_ref, width):
    half_rows = rows_ref.shape[0] // 2
    pick = pick_rows(half_rows, 4)
    tails = []
    for h in range(2):
        at = slice(h * half_rows, (h + 1) * half_rows)
        for start, stop in chunks(width):
            part = load_half(in_ref, h, start, stop, width)
            rows_ref[at, start:stop] = dot(pick, part, ((1,), (0,))).astype(BF16)
        tails.append(load_half_stats(in_ref, h, 2 * width))
        moved = dot(pick, tails[h].astype(BF16), ((1,), (0,)))
        rows_ref[at, width : width + LANES] = moved.astype(BF16)
    return tails


def fold(block, pieces):
    return jnp.concatenate(
        [block[c * pieces : (c + 1) * pieces, :] for c in range(block.shape[0] // pieces)], axis=1
    )


def unfold(rows):
    return jnp.concatenate(
        [rows[:, c * LANES : (c + 1) * LANES] for c in range(rows.shape[1] // LANES)], axis=0
    )


def pack_kernel(
    partner_hbm,
    q_hbm,
    k_hbm,
    g_hbm,
    delta_hbm,
    out_hbm,
    summary_ref,
    out_ref,
    rows_ref,
    partner_ref,
    q_ref,
    k_ref,
    g_ref,
    delta_ref,
    sems,
    small_sems,
    out_sems,
):
    blocks, pieces, block_len = 8, 64, 256
    score_scale = 1.0 / math.sqrt(HALF)
    pool_scale = 1.0 / math.sqrt(block_len)
    copies = []
    for half in range(2):
        at = pl.ds(half * blocks // 2 * block_len, blocks // 2 * block_len)
        pairs = ((k_hbm, k_ref), (q_hbm, q_ref))
        copies.append(
            [
                pltpu.make_async_copy(there.at[at], here.at[at], sems.at[half, i])
                for i, (there, here) in enumerate(pairs)
            ]
        )
    copies[1].append(pltpu.make_async_copy(g_hbm, g_ref, sems.at[0, 2]))
    copies[0] += [
        pltpu.make_async_copy(delta_hbm, delta_ref, small_sems.at[0]),
        pltpu.make_async_copy(partner_hbm, partner_ref, small_sems.at[1]),
    ]
    for copy in copies[0] + copies[1]:
        copy.start()

    tails, sent = [], []
    for j in range(blocks):
        if j % (blocks // 2) == 0:
            for copy in copies[j // (blocks // 2)]:
                copy.wait()
        at = slice(j * block_len, (j + 1) * block_len)
        qb, kb = q_ref[at, :], k_ref[at, :]
        scores = dot(kb, head_stack(qb, score_scale), ((1,), (1,)))
        top = jnp.max(scores, axis=0, keepdims=True)
        lse = top + jnp.log(jnp.sum(jnp.exp(scores - top), axis=0, keepdims=True))
        summary = jnp.sum(kb.astype(F32), axis=0, keepdims=True) * pool_scale
        summary_ref[j : j + 1, :] = summary
        delta = jnp.concatenate([delta_ref[0:1, at], delta_ref[1:2, at]], axis=1)
        left = jnp.concatenate(
            list(split3(narrow(to_rows(lse))))
            + list(split3(narrow(head_rows(summary))))
            + [jnp.zeros((4, QUARTER), F32)],
            axis=0,
        )
        deltas = jnp.concatenate(split3(narrow(narrow(to_rows(delta))))[:2], axis=0)
        lane = lax.broadcasted_iota(jnp.int32, (pieces, LANES - TAGS), 1)
        place = partner_ref[j]
        high = ((place & 4) << 4) | (place >> 3)
        tags = jnp.where(
            lane == 0,
            high.astype(F32),
            jnp.where(lane == 1, (place & 3).astype(F32), 0.0),
        )
        to = slice(j * pieces, (j + 1) * pieces)
        rows_ref[to, 0:512] = fold(qb, pieces)
        for other in range(j + 1 if j == blocks // 2 else 0):
            gb = g_ref[other * block_len : (other + 1) * block_len, :]
            rows_ref[other * pieces : (other + 1) * pieces, 512:1024] = fold(gb, pieces)
        if j > blocks // 2:
            rows_ref[to, 512:1024] = fold(g_ref[at, :], pieces)
        rows_ref[to, 1024:1152] = jnp.concatenate([left, deltas, tags], axis=1).astype(BF16)

        if j == blocks // 2:
            tails.append(send_half(out_ref, rows_ref, 1024, 0))
            sent.append(
                pltpu.make_async_copy(
                    out_ref.at[:, :, pl.ds(0, 1024)],
                    out_hbm.at[:, :, pl.ds(0, 1024)],
                    out_sems.at[0],
                )
            )
            sent[0].start()
    tails.append(send_half(out_ref, rows_ref, 1024, 1))
    store_stats(out_ref, 2048, *tails)
    sent.append(
        pltpu.make_async_copy(
            out_ref.at[:, :, pl.ds(1024, 1152)],
            out_hbm.at[:, :, pl.ds(1024, 1152)],
            out_sems.at[1],
        )
    )
    sent[1].start()
    for copy in sent:
        copy.wait()


def partner_pick(place):
    rows = place.shape[1]
    row = lax.broadcasted_iota(jnp.int32, (rows, rows), 0).astype(F32)
    return jnp.where(row == place, 1.0, 0.0).astype(BF16)


def forward_kernel(in_ref, out_ref, place_ref):
    tail = jnp.concatenate([load_half_stats(in_ref, h, 2048) for h in range(2)], axis=0)
    tags = tail.T
    place = tags[TAGS : TAGS + 1, :] * 4.0 + tags[TAGS + 1 : TAGS + 2, :]
    place_ref[...] = place
    pick = partner_pick(place)
    half_rows = tail.shape[0] // 2
    for start, stop in chunks(1024):
        part = jnp.concatenate(
            [load_half(in_ref, h, start, stop, 1024) for h in range(2)], axis=0
        )
        moved = dot(pick, part, ((1,), (0,)))
        store_half(out_ref, 0, moved[:half_rows], start, stop, 1024)
        store_half(out_ref, 1, moved[half_rows:], start, stop, 1024)
    moved = dot(pick, tail.astype(BF16), ((1,), (0,)))
    store_stats(out_ref, 2048, moved[:half_rows], moved[half_rows:])


def backward_kernel(place_ref, in_ref, out_ref):
    pick = partner_pick(place_ref[...])
    half_rows = pick.shape[0] // 2
    for start, stop in chunks(512):
        part = jnp.concatenate(
            [load_half(in_ref, h, start, stop, 512) for h in range(2)], axis=0
        )
        moved = dot(pick, part, ((0,), (0,)))
        store_half(out_ref, 0, moved[:half_rows], start, stop, 512)
        store_half(out_ref, 1, moved[half_rows:], start, stop, 512)
    tails = [load_half_stats(in_ref, h, 1024) for h in range(2)]
    moved = dot(pick, jnp.concatenate(tails, axis=0).astype(BF16), ((0,), (0,)))
    lane8 = lax.broadcasted_iota(jnp.int32, (8, LANES), 1)
    lane = lax.broadcasted_iota(jnp.int32, (half_rows, LANES), 1)
    sent = []
    for h in range(2):
        total = jnp.sum(tails[h].reshape(half_rows // 8, 8, LANES), axis=0)
        total = total + pltpu.roll(total, 4, 0)
        total = total + pltpu.roll(total, LANES - SHARE, 1)
        total = jnp.where((lane8 >= QUARTER) & (lane8 < QUARTER + SHARE), total, 0.0)
        high, mid, _ = split3(total)
        share = high + pltpu.roll(mid, SHARE, 1)
        share = jnp.broadcast_to(share[None], (half_rows // 8, 8, LANES))
        share = share.reshape(half_rows, LANES)
        at = slice(h * half_rows, (h + 1) * half_rows)
        sent.append(jnp.where(lane < QUARTER, moved[at], share))
    store_stats(out_ref, 1024, *sent)


def far_kernel(
    in_ref,
    k_ref,
    v_ref,
    summary_ref,
    w_ref,
    out_ref,
    dk_ref,
    dv_ref,
    column_ref,
    rows_ref,
    back_ref,
    gate_ref,
    grad_ref,
):
    blocks, pieces, block_len = 8, 64, 256
    score_scale = 1.0 / math.sqrt(HALF)
    receive_rows(rows_ref, in_ref, 1024)
    arrived = []
    for j in range(blocks):
        s = rows_ref[j * pieces + 48 : (j + 1) * pieces, 1024:1152].astype(F32)[:, :QUARTER]
        arrived.append(from_head_rows(widen(s[0:4] + s[4:8] + s[8:12])))
    summary_in = jnp.concatenate(arrived, axis=0)
    summary = summary_ref[...]
    sortq = dot(summary_in, block_diagonal(w_ref), ((1,), (0,)), precision=lax.Precision.HIGHEST)
    gates = jax.nn.sigmoid(score_scale * head_sums(sortq * summary))
    gate_ref[...] = gates

    def step(j, carry):
        at = pl.ds(pl.multiple_of(j * block_len, block_len), block_len)
        here = pl.ds(pl.multiple_of(j * pieces, pieces), pieces)
        kb, vb = k_ref[at, :], v_ref[at, :]
        qs = head_stack(unfold(rows_ref[here, 0:512]), score_scale)
        gs = head_stack(unfold(rows_ref[here, 512:1024]), 1.0)
        stats = rows_ref[here, 1024:1152].astype(F32)
        parts = stats[:, :QUARTER]
        own_lse = from_rows(widen(parts[0:16] + parts[16:32] + parts[32:48]))
        parts = stats[:, QUARTER:TAGS]
        delta = from_rows(widen(widen(parts[0:32] + parts[32:64])))
        gate = gate_ref[pl.ds(j, 1), :]
        gate_row = jnp.concatenate(
            [
                jnp.broadcast_to(gate[:, 0:1], (1, block_len)),
                jnp.broadcast_to(gate[:, HALF : HALF + 1], (1, block_len)),
            ],
            axis=1,
        )
        scores = dot(kb, qs, ((1,), (1,)))
        top = jnp.maximum(own_lse, jnp.max(scores, axis=0, keepdims=True))
        weights = jnp.exp(scores - top)
        total = jnp.exp(own_lse - top) + jnp.sum(weights, axis=0, keepdims=True)
        probs = weights * (1.0 / total)
        lse = top + jnp.log(total)
        low = probs.astype(BF16)
        dprobs = dot(vb, gs, ((1,), (1,)))
        dscores = (probs * (gate_row * dprobs - delta)).astype(BF16)
        dk_ref[at, :] = dot(dscores, qs, ((1,), (0,))).astype(BF16)
        dv = dot(low, gs, ((1,), (0,)))
        dv_ref[at, :] = (dv * gate).astype(BF16)
        grad_ref[pl.ds(j, 1), :] = jnp.sum(dv * vb.astype(F32), axis=0, keepdims=True)
        dq = dot(kb, dscores, ((0,), (0,))) * score_scale
        dq = jnp.concatenate([dq[:HALF, :block_len], dq[HALF:, block_len:]], axis=1)
        back_ref[here, 0:512] = dq.astype(BF16)
        parts = jnp.concatenate(
            list(split3(narrow(to_rows(lse)))) + [jnp.zeros((16, QUARTER), F32)], axis=0
        )
        back_ref[here, 512:640] = jnp.concatenate(
            [parts, jnp.zeros((pieces, LANES - QUARTER), F32)], axis=1
        ).astype(BF16)
        return carry

    lax.fori_loop(0, blocks, step, 0, unroll=True)
    logit_grad = head_sums(grad_ref[...]) * gates * (1.0 - gates)
    sortq_grad = score_scale * logit_grad * summary
    column_ref[...] = score_scale * logit_grad * sortq
    for j in range(blocks):
        parts = jnp.concatenate(
            list(split3(narrow(head_rows(sortq_grad[j : j + 1, :]))))
            + [jnp.zeros((4, QUARTER), F32)],
            axis=0,
        )
        back_ref[j * pieces + 48 : (j + 1) * pieces, 512:640] = jnp.concatenate(
            [parts, jnp.zeros((16, LANES - QUARTER), F32)], axis=1
        ).astype(BF16)
    outer = dot(summary_in, sortq_grad, ((0,), (0,)), precision=lax.Precision.HIGHEST)
    lane = lax.broadcasted_iota(jnp.int32, (LANES, LANES), 1)
    row = lax.broadcasted_iota(jnp.int32, (LANES, LANES), 0)
    outer = jnp.where(row < HALF, outer, pltpu.roll(outer, HALF, 1))
    inside = (lane >= QUARTER) & (lane < QUARTER + SHARE)
    shares = []
    for a in range(4):
        part = jnp.where(inside, pltpu.roll(outer, (QUARTER - SHARE * a) % LANES, 1), 0.0)
        high, mid, _ = split3(part)
        shares.append(high + pltpu.roll(mid, SHARE, 1))
    extra = [jnp.concatenate(shares[2 * h : 2 * h + 2], axis=0) for h in range(2)]
    send_rows(out_ref, back_ref, 512, extra)


def self_kernel(
    in_ref,
    q_ref,
    k_ref,
    v_ref,
    g_ref,
    delta_ref,
    w_ref,
    dk_far_ref,
    dv_far_ref,
    column_ref,
    dq_hbm,
    dk_hbm,
    dv_hbm,
    sort_out,
    rows_ref,
    dq_out,
    dk_out,
    dv_out,
    sems,
):
    blocks, pieces, block_len = 8, 64, 256
    score_scale = 1.0 / math.sqrt(HALF)
    pool_scale = 1.0 / math.sqrt(block_len)
    tails = receive_rows(rows_ref, in_ref, 512)
    arrived = []
    for j in range(blocks):
        s = rows_ref[j * pieces + 48 : (j + 1) * pieces, 512:640].astype(F32)[:, :QUARTER]
        arrived.append(from_head_rows(widen(s[0:4] + s[4:8] + s[8:12])))
    sortq_grad = jnp.concatenate(arrived, axis=0)
    row_grad = dot(
        sortq_grad, block_diagonal(w_ref), ((1,), (1,)), precision=lax.Precision.HIGHEST
    )
    extra = pool_scale * (row_grad + column_ref[...])

    lane = lax.broadcasted_iota(jnp.int32, (LANES, LANES), 1)
    found = jnp.zeros((LANES, LANES), F32)
    for a in range(4):
        s = tails[a // 2][(a % 2) * LANES : (a % 2 + 1) * LANES]
        s = s + pltpu.roll(s, LANES - SHARE, 1)
        s = pltpu.roll(s, (SHARE * a - QUARTER) % LANES, 1)
        inside = (lane >= SHARE * a) & (lane < SHARE * (a + 1))
        found = found + jnp.where(inside, s, 0.0)
    sort_out[...] = found[:, :HALF]

    copies = []
    for j in range(blocks):
        at = slice(j * block_len, (j + 1) * block_len)
        here = slice(j * pieces, (j + 1) * pieces)
        kb, vb = k_ref[at, :], v_ref[at, :]
        qs = head_stack(q_ref[at, :], score_scale)
        gs = head_stack(g_ref[at, :], 1.0)
        far = rows_ref[here, 0:512].astype(F32)
        stats = rows_ref[here, 512:640].astype(F32)
        stats = stats[:, :QUARTER]
        lse = from_rows(widen(stats[0:16] + stats[16:32] + stats[32:48]))
        delta = jnp.concatenate([delta_ref[0:1, at], delta_ref[1:2, at]], axis=1)
        scores = dot(kb, qs, ((1,), (1,)))
        probs = jnp.exp(scores - lse)
        low = probs.astype(BF16)
        dprobs = dot(vb, gs, ((1,), (1,)))
        dscores = (probs * (dprobs - delta)).astype(BF16)
        dk = dot(dscores, qs, ((1,), (0,)))
        dk_out[at, :] = (dk + dk_far_ref[at, :].astype(F32) + extra[j : j + 1, :]).astype(BF16)
        dv = dot(low, gs, ((1,), (0,)))
        dv_out[at, :] = (dv + dv_far_ref[at, :].astype(F32)).astype(BF16)
        dq = dot(kb, dscores, ((0,), (0,))) * score_scale
        dq = jnp.concatenate(
            [
                dq[:HALF, :block_len] + far[:, :block_len],
                dq[HALF:, block_len:] + far[:, block_len:],
            ],
            axis=0,
        )
        dq_out[at, :] = dq.T.astype(BF16)
        if j % (blocks // 2) == blocks // 2 - 1:
            half = j // (blocks // 2)
            rows = pl.ds(half * blocks // 2 * block_len, blocks // 2 * block_len)
            pairs = ((dq_out, dq_hbm), (dk_out, dk_hbm), (dv_out, dv_hbm))
            for i, (here_ref, there) in enumerate(pairs):
                copy = pltpu.make_async_copy(here_ref.at[rows], there.at[rows], sems.at[half, i])
                copy.start()
                copies.append(copy)

    for copy in copies:
        copy.wait()


def whole(memory_space=pltpu.VMEM):
    return pl.BlockSpec(memory_space=memory_space)


def call(
    kernel, outs, inputs, scratch=(), in_hbm=False, out_hbm=0, limit=VMEM_LIMIT, flops=1 << 28
):
    shapes = [jax.ShapeDtypeStruct(shape, dtype) for shape, dtype in outs]
    size = sum(math.prod(s.shape) * s.dtype.itemsize for s in shapes)
    size += sum(x.size * x.dtype.itemsize for x in inputs)
    return pl.pallas_call(
        kernel,
        out_shape=shapes,
        in_specs=[whole(pl.ANY if in_hbm else pltpu.VMEM)] * len(inputs),
        out_specs=[whole(pl.ANY)] * out_hbm + [whole()] * (len(shapes) - out_hbm),
        scratch_shapes=list(scratch),
        compiler_params=pltpu.CompilerParams(vmem_limit_bytes=limit),
        cost_estimate=pl.CostEstimate(flops=flops, bytes_accessed=size, transcendentals=1 << 20),
    )(*inputs)


def exchange(x):
    return lax.all_to_all(x, "seq", split_axis=0, concat_axis=0, tiled=True)


def per_device(queries, keys, values, delta, dout, partner, sort_weight):
    tokens = queries.shape[0]
    rows = lax.axis_size("seq") * partner.shape[0]
    blocks = partner.shape[0]
    buffer = pltpu.VMEM((tokens, LANES), BF16)
    wide_slots = ((rows // blocks, 4, 2176), BF16)
    sent, summary = call(
        pack_kernel,
        [wide_slots, ((blocks, LANES), F32)],
        [partner, queries, keys, dout, delta],
        scratch=[
            pltpu.VMEM(wide_slots[0], BF16),
            pltpu.VMEM((rows, 1152), BF16),
            pltpu.SMEM((blocks,), jnp.int32),
            buffer,
            buffer,
            buffer,
            pltpu.VMEM(delta.shape, F32),
            pltpu.SemaphoreType.DMA((2, 3)),
            pltpu.SemaphoreType.DMA((2,)),
            pltpu.SemaphoreType.DMA((2,)),
        ],
        in_hbm=True,
        out_hbm=1,
        limit=WHOLE_LIMIT,
    )
    spread = exchange(sent)
    moved, place = call(
        forward_kernel, [wide_slots, ((1, rows), F32)], [spread]
    )
    arrived = exchange(moved)
    slots = ((rows // blocks, 4, 1152), BF16)
    back, dk_far, dv_far, column = call(
        far_kernel,
        [
            slots,
            ((tokens, LANES), BF16),
            ((tokens, LANES), BF16),
            ((8, LANES), F32),
        ],
        [arrived, keys, values, summary, sort_weight],
        scratch=[
            pltpu.VMEM((rows, 1152), BF16),
            pltpu.VMEM((rows, 640), BF16),
            pltpu.VMEM((8, LANES), F32),
            pltpu.VMEM((8, LANES), F32),
        ],
    )
    spread_back = exchange(back)
    (moved_back,) = call(backward_kernel, [slots], [place, spread_back])
    arrived_back = exchange(moved_back)
    d_queries, d_keys, d_values, d_sort = call(
        self_kernel,
        [((tokens, LANES), BF16)] * 3 + [((LANES, HALF), F32)],
        [
            arrived_back,
            queries,
            keys,
            values,
            dout,
            delta,
            sort_weight,
            dk_far,
            dv_far,
            column,
        ],
        scratch=[
            pltpu.VMEM((rows, 640), BF16),
            buffer,
            buffer,
            buffer,
            pltpu.SemaphoreType.DMA((2, 3)),
        ],
        out_hbm=3,
    )
    return d_queries, d_keys, d_values, d_sort.reshape(sort_weight.shape)


def solution(mesh):
    in_specs = (
        P("seq", "head"),
        P("seq", "head"),
        P("seq", "head"),
        P("head", "seq"),
        P("seq", "head"),
        P("seq"),
        P("head", None, None),
    )
    out_specs = (P("seq", "head"), P("seq", "head"), P("seq", "head"), P("head", None, None))
    return jax.shard_map(
        per_device, mesh=mesh, in_specs=in_specs, out_specs=out_specs, check_vma=False
    )
```
